512 devices in a mesh: gx: 2 (over core), gy: 2 (over x_lo), gz: 128 (over z, y, x_hi).
Axes of the slice: x: 4 (x_hi: 2, x_lo: 2; x = x_hi * 2 + x_lo), y: 8, z: 8, core: 2. Of those that a mesh axis runs over, the one named last changes fastest.
Arguments:
- populations: bfloat16 [7, 4, 2, 128, 32768], P(None, 'gx', 'gy', 'gz'), may hold values from 0 to 0.25
- adjoint_final: bfloat16 [7, 4, 2, 128, 32768], P(None, 'gx', 'gy', 'gz'), may hold values from -6 to 6
- velocity: bfloat16 [3, 4, 2, 128, 32768], P(None, 'gx', 'gy', 'gz'), may hold values from -0.14941406 to 0.14941406
- particle_kappa: float32 [4, 2, 128, 32768], P('gx', 'gy', 'gz'), may hold values from 0.02 to 0.3
- solid_label: int32 [4, 2, 128, 32768], P('gx', 'gy', 'gz'), may hold values 0 or 1
- tile_active: int32 [4, 2, 128], P('gx', 'gy', 'gz'), may hold values 0 or 1
Outputs:
- adjoint_first: float32 [7, 4, 2, 128, 32768], P(None, 'gx', 'gy', 'gz')
- kappa_gradient: float32 [4, 2, 128, 32768], P('gx', 'gy', 'gz')
The draws below stay inside these ranges and needn't reach their ends.
All inputs are finite; a program needn't handle non-finite values. No bound on the sum of `solid_label` or of `tile_active` on one device may be relied on, other than what follows from the above.
Results may differ from the reference program's by a relative error of at most 0.00045.
Values sent between devices are 32-bit elements; how exact they have to be, the bound alone decides.
A program may use at most 64 MiB of HBM per device.

```python
import math
import jax
import jax.numpy as jnp
from jax import lax

EDGE = 32
TX = 4
TY = 2
TZ = 128
CELLS = 32768


def plant(values, rng, smallest, top_value):
    spot = [jax.random.randint(jax.random.fold_in(rng, axis), (), 0, length) for axis, length in enumerate(values.shape)]
    widest = values.shape.index(max(values.shape))
    neighbour = spot[:widest] + [(spot[widest] + 1) % values.shape[widest]] + spot[widest + 1:]
    return values.at[tuple(spot)].set(smallest).at[tuple(neighbour)].set(top_value)


def levels(rng, dims, split, smallest, top_value):
    def one(dim, parts):
        steps = jax.random.uniform(jax.random.fold_in(jax.random.fold_in(rng, 6), dim), (parts,), jnp.float32, smallest / len(split), top_value / len(split))
        return jnp.repeat(jnp.exp(steps), dims[dim] // parts).reshape((-1,) + (1,) * (len(dims) - dim - 1))

    level = one(*split[0])
    for cut in split[1:]:
        level = level * one(*cut)
    return level


def gaussian(own_key, shape, spread, limit, pieces=(), kind=jnp.bfloat16):
    factor_of = levels(own_key, shape, pieces, -0.22, 0.18) if pieces else 1.0
    array = jax.random.normal(own_key, shape, jnp.float32) * spread * factor_of
    return jnp.minimum(jnp.maximum(array, -limit), limit).astype(kind)


def setup_inputs(seed: int = 0) -> dict:
    arg_keys = jax.random.split(jax.random.key(seed), 7)
    populations = jnp.clip(0.25 * jax.random.uniform(arg_keys[0], (7, TX, TY, TZ, CELLS), jnp.float32) ** levels(arg_keys[0], (7, TX, TY, TZ, CELLS), ((1, 2), (2, 2), (3, 128)), -0.2, 0.2), 0.0, 0.25).astype(jnp.bfloat16)
    adjoint_final = gaussian(arg_keys[1], (7, TX, TY, TZ, CELLS), 1.0, 6.0, ((1, 2), (2, 2), (3, 128)))
    velocity = jnp.clip(jax.random.uniform(arg_keys[2], (3, TX, TY, TZ, CELLS), jnp.float32, -0.14941406, 0.14941406) * levels(arg_keys[2], (3, TX, TY, TZ, CELLS), ((1, 2), (2, 2), (3, 128)), -0.4, 0.0), -0.14941406, 0.14941406).astype(jnp.bfloat16)
    particle_kappa = jnp.clip(jnp.exp(math.log(0.3) - 2.7080503 * jax.random.uniform(arg_keys[3], (TX, TY, TZ, CELLS), jnp.float32) ** levels(arg_keys[3], (TX, TY, TZ, CELLS), ((0, 2), (1, 2), (2, 128)), -0.2, 0.2)), 0.02, 0.3)
    solid_label = plant((jax.random.randint(arg_keys[4], (TX, TY, TZ, CELLS), 0, 5) < 2).astype(jnp.int32), jax.random.fold_in(arg_keys[4], 1), 0, 1)
    tile_active = plant((jax.random.randint(arg_keys[5], (TX, TY, TZ), 0, 4) < 3).astype(jnp.int32), jax.random.fold_in(arg_keys[5], 1), 0, 1)
    return {"populations": populations, "adjoint_final": adjoint_final, "velocity": velocity, "particle_kappa": particle_kappa, "solid_label": solid_label, "tile_active": tile_active}


DIRECTIONS = ((0, 0), (0, 1), (0, -1), (1, 1), (1, -1), (2, 1), (2, -1))
FLUID_KAPPA = 1.0 / 6.0


def to_grid(tiles):
    count, tile_x, tile_y, tile_z, voxels = tiles.shape
    shaped = tiles.reshape(count, tile_x, tile_y, tile_z, EDGE, EDGE, EDGE)
    shaped = shaped.transpose(0, 1, 4, 2, 5, 3, 6)
    return shaped.reshape(count, tile_x * EDGE, tile_y * EDGE, tile_z * EDGE)


def to_tiles(grid):
    count, size_x, size_y, size_z = grid.shape
    tile_x, tile_y, tile_z = size_x // EDGE, size_y // EDGE, size_z // EDGE
    shaped = grid.reshape(count, tile_x, EDGE, tile_y, EDGE, tile_z, EDGE)
    shaped = shaped.transpose(0, 1, 3, 5, 2, 4, 6)
    return shaped.reshape(count, tile_x, tile_y, tile_z, EDGE * EDGE * EDGE)


def factor(number, drift):
    if number == 0:
        return 0.25
    dim, sign = DIRECTIONS[number]
    return 0.125 * (1.0 + 4.0 * sign * drift[dim])


def moved(values, dim, sign):
    extent = values.shape[dim]
    zero = jnp.zeros_like(lax.slice_in_dim(values, 0, 1, axis=dim))
    if sign > 0:
        return jnp.concatenate([zero, lax.slice_in_dim(values, 0, extent - 1, axis=dim)], dim)
    return jnp.concatenate([lax.slice_in_dim(values, 1, extent, axis=dim), zero], dim)


def stream(field, flip):
    result = [field[0]]
    for number in range(1, 7):
        dim, sign = DIRECTIONS[number]
        result.append(moved(field[number], dim, sign * flip))
    return jnp.stack(result)


def adjoint_step(adjoint_next, state, relax_rate, drift, active):
    pulled = stream(adjoint_next, -1)
    weighted = factor(0, drift) * pulled[0]
    for number in range(1, 7):
        weighted = weighted + factor(number, drift) * pulled[number]
    adjoint_prev = active * ((1.0 - relax_rate) * pulled + relax_rate * weighted)
    term = active * (weighted * jnp.sum(state, axis=0) - jnp.sum(pulled * state, axis=0))
    return adjoint_prev, term


def reference(populations, adjoint_final, velocity, particle_kappa, solid_label, tile_active):
    active = tile_active.astype(jnp.float32)
    active = jnp.repeat(jnp.repeat(jnp.repeat(active, EDGE, axis=0), EDGE, axis=1), EDGE, axis=2)
    solid = to_grid(solid_label[None])[0].astype(jnp.float32)
    kappa = jnp.where(solid > 0.5, to_grid(particle_kappa[None])[0], FLUID_KAPPA)
    relax_rate = 1.0 / (4.0 * kappa + 0.5)
    drift = to_grid(velocity).astype(jnp.float32) * (1.0 - solid)
    state_first = to_grid(populations).astype(jnp.float32)
    total_first = jnp.sum(state_first, axis=0)
    post = jnp.stack([active * (state_first[number] - relax_rate * (state_first[number] - factor(number, drift) * total_first)) for number in range(7)])
    state_second = stream(post, 1)
    adjoint_middle, term_second = adjoint_step(to_grid(adjoint_final).astype(jnp.float32), state_second, relax_rate, drift, active)
    adjoint_first, term_first = adjoint_step(adjoint_middle, state_first, relax_rate, drift, active)
    gradient = solid * (-4.0 * relax_rate * relax_rate) * (term_second + term_first)
    return to_tiles(adjoint_first), to_tiles(gradient[None])[0]
```

```python
import functools

import jax
import jax.numpy as jnp
from jax import lax
from jax.experimental import pallas as pl
from jax.experimental.pallas import tpu as pltpu
from jax.sharding import PartitionSpec as P

EDGE = 32
FLUID_KAPPA = 1.0 / 6.0
MESH = pl.DeviceIdType.MESH
F32 = jnp.float32
LAYERS = 2 * EDGE
ROWS = 8 * LAYERS
PARTS = (6, 11, 10, 10, 2, 2, 2, 3, 3)


def masks():
    lane = lax.broadcasted_iota(jnp.int32, (8, 128), 1)
    sub = lax.broadcasted_iota(jnp.int32, (8, 128), 0)
    return lane & 31, lane >> 5, sub


def pick(flag, yes, no):
    return jnp.where(jnp.broadcast_to(flag, (8, 128)), yes, no)


def z_up(v, halo, kz):
    return jnp.where(kz == 31, halo, pltpu.roll(v, 127, 1))


def z_down(v, halo, kz):
    return jnp.where(kz == 0, halo, pltpu.roll(v, 1, 1))


def y_up(v, halo, grp, sub):
    r = pltpu.roll(v, 96, 1)
    inner = jnp.where(grp == 3, pltpu.roll(r, 7, 0), r)
    return jnp.where((grp == 3) & (sub == 7), halo, inner)


def y_down(v, halo, grp, sub):
    r = pltpu.roll(v, 32, 1)
    inner = jnp.where(grp == 0, pltpu.roll(r, 1, 0), r)
    return jnp.where((grp == 0) & (sub == 0), halo, inner)


def weighted(q, d):
    even = (q[1] + q[2]) + (q[3] + q[4]) + (q[5] + q[6])
    odd = d[0] * (q[1] - q[2]) + d[1] * (q[3] - q[4]) + d[2] * (q[5] - q[6])
    return 0.25 * q[0] + 0.125 * even + 0.5 * odd


def tile8(row):
    return pl.ds(pl.multiple_of(row, 8), 8)


def exchange(
    nz, pop_h, fin_h, vel_h, kap_h, sol_h, act_h,
    tf, tg, po, co, yh, zh, xh,
    popb, finb, velb, kapb, solb, actb, tv, zm, ym, zp,
    s0, s1, s2, s3, s4, s5, s6, s7, s8, r0, r1, r2, r3, r4, r5, r6, r7, r8,
    load_sem, send_sem, recv_sem,
):
    sends = (s0, s1, s2, s3, s4, s5, s6, s7, s8)
    gets = (r0, r1, r2, r3, r4, r5, r6, r7, r8)
    gx, gy, gz = lax.axis_index("gx"), lax.axis_index("gy"), lax.axis_index("gz")
    ox, oy, up, down = 1 - gx, 1 - gy, gz + 1, gz - 1
    peers = (
        (ox, gy, gz), (gx, oy, gz), (gx, gy, up), (gx, gy, down), (ox, oy, gz),
        (ox, gy, up), (ox, gy, down), (gx, oy, up), (gx, oy, down),
    )
    has_up, has_down = gz < nz - 1, gz > 0
    exists = (None, None, has_up, has_down, None, has_up, has_down, has_up, has_down)

    def guarded(k, act):
        if exists[k] is None:
            act()
        else:
            pl.when(exists[k])(act)

    barrier = pltpu.get_barrier_semaphore()
    for k in range(9):
        guarded(k, lambda k=k: pl.semaphore_signal(barrier, inc=1, device_id=peers[k], device_id_type=MESH))
    loads = [
        pltpu.make_async_copy(src, dst, load_sem.at[n])
        for n, (src, dst) in enumerate(
            ((act_h, actb), (fin_h, finb), (vel_h, velb), (kap_h, kapb), (sol_h, solb), (pop_h, popb))
        )
    ]
    for copy in loads:
        copy.start()

    kz, grp, sub = masks()
    zero = jnp.zeros((8, 128), F32)
    s_e, g_e = 7 * oy, 3 * oy
    s_c = lax.rem(s_e + 4, 8)
    i_e, p_e = 31 * ox, ox
    sgx, sgy = (1 - 2 * gx).astype(F32), (1 - 2 * gy).astype(F32)
    first_x, first_y = gx == 0, gy == 0
    fx, fy, bx, by = 1 + ox, 3 + oy, 1 + gx, 3 + gy
    zsign = jnp.where(kz == 0, -0.5, 0.5)

    @pl.when(gz == nz - 1)
    def _():
        for k in (2, 5, 7):
            gets[k][...] = jnp.zeros_like(gets[k])

    @pl.when(gz == 0)
    def _():
        for k in (3, 6, 8):
            gets[k][...] = jnp.zeros_like(gets[k])

    loads[1].wait()
    for n in range(7):
        tf[n, 16 : 16 + ROWS, :] = finb[n].astype(F32)
    for n in (1, 2):
        tf[n, pl.ds(0, 8, stride=2), :] = zero
        tf[n, pl.ds(1, 8, stride=2), :] = tf[n, pl.ds(16 * 32, 8, stride=2), :]
        tf[n, pl.ds(16 * 33, 8, stride=2), :] = tf[n, pl.ds(16 + 1, 8, stride=2), :]
        tf[n, pl.ds(16 * 33 + 1, 8, stride=2), :] = zero
        po[n, 0:8, :] = zero
        po[n, ROWS + 8 : ROWS + 16, :] = zero
    loads[2].wait()
    for n in range(3):
        tv[n] = velb[n].astype(F32)
    loads[5].wait()
    for n in range(7):
        tg[n] = popb[n].astype(F32)
    loads[0].wait()
    loads[3].wait()
    loads[4].wait()
    active = (actb[0, 0].astype(F32), actb[0, 1].astype(F32))

    def cell(i, p, a):
        near = [tf[n, pl.ds(16 * (i + 1) + p, 8, stride=2), :] for n in (0, 3, 4, 5, 6)]
        q = [
            near[0],
            tf[1, pl.ds(16 * (i + 2) + p, 8, stride=2), :],
            tf[2, pl.ds(16 * i + p, 8, stride=2), :],
            y_up(near[1], zero, grp, sub),
            y_down(near[2], zero, grp, sub),
            z_up(near[3], zero, kz),
            z_down(near[4], zero, kz),
        ]
        here = tile8(256 * p + 8 * i)
        solid = solb[here, :] > 0
        kappa = jnp.where(solid, kapb[here, :], FLUID_KAPPA)
        rate = 1.0 / (4.0 * kappa + 0.5)
        ar = a * rate
        b = a - ar
        d = [jnp.where(solid, 0.0, tv[n, pl.ds(16 * i + p, 8, stride=2), :]) for n in range(3)]
        return near, q, solid, rate, ar, b, d, ar * weighted(q, d)

    def layer(i, p):
        x = 32 * p + i
        near, q, solid, rate, ar, b, d, ars = cell(i, p, active[p])
        here = tile8(8 * x)
        padded = tile8(8 * x + 8)
        for n, c in enumerate((ar, b, d[0], d[1], d[2])):
            co[n, here, :] = c
        co[5, here, :] = jnp.where(solid, -4.0 * active[p] * rate * rate, 0.0)
        g = [tg[n, pl.ds(16 * i + p, 8, stride=2), :] for n in range(7)]
        total = ((g[0] + g[1]) + (g[2] + g[3])) + ((g[4] + g[5]) + g[6])
        w = ar * total
        post = [b * g[0] + 0.25 * w]
        for n in range(3):
            even, odd = 0.125 * w, 0.5 * (w * d[n])
            post.append(b * g[2 * n + 1] + (even + odd))
            post.append(b * g[2 * n + 2] + (even - odd))
        for n in range(7):
            po[n, padded, :] = post[n]
        to_y = ar * (0.125 + 0.5 * sgy * d[1])
        bottom = kz == 0
        zm[0, here, :] = jnp.where(bottom, near[3], near[4])
        zm[1, here, :] = jnp.where(bottom, post[6], post[5])
        zm[2, here, :] = ars + b * jnp.where(bottom, q[5], q[6])
        zm[3, here, :] = ar * (0.125 + zsign * d[2])
        zm[4, here, :] = jnp.where(sub == s_e, pick(first_y, near[2], near[1]), pltpu.roll(to_y, 4, 0))
        ym[0, here, :] = ars + b * pick(first_y, q[4], q[3])
        ym[1, here, :] = to_y

    def sweep(i, carry):
        layer(i, 0)
        layer(i, 1)
        return carry

    lax.fori_loop(0, 32, sweep, 0)

    a_e = jnp.where(first_x, active[1], active[0])
    near, q, solid, rate, ar, b, d, ars = cell(i_e, p_e, a_e)
    x_e = 63 * ox
    here_e = tile8(8 * x_e)
    to_x = ar * (0.125 + 0.5 * sgx * d[0])
    own_x = tf[fx, pl.ds(16 * (i_e + 1) + p_e, 8, stride=2), :]
    own_y = pick(first_y, near[2], near[1])
    s0[0] = own_x
    s0[1] = po[bx, tile8(8 * x_e + 8), :]
    s0[2] = ars + b * pick(first_x, q[2], q[1])
    s0[3] = to_x
    s0[4] = ym[1, here_e, :]
    s0[5] = zm[3, here_e, :]

    def pack_y(read):
        out = []
        for h in range(2):
            v = zero
            for g in range(4):
                rows = read(32 * h + 8 * g, h, 8 * g)
                v = jnp.where(grp == g, pltpu.roll(rows, lax.rem(32 * (g - g_e) + 128, 128), 1), v)
            out.append(v)
        return out

    def every8(ref, n, pad):
        return lambda x, h, i: ref[n, pl.ds(8 * (x + pad) + s_e, 8, stride=8), :]

    packs = (
        pack_y(lambda x, h, i: tf[fy, pl.ds(16 * (i + 1) + h + 2 * s_e, 8, stride=16), :]),
        pack_y(every8(po, by, 1)),
        pack_y(every8(ym, 0, 0)),
        pack_y(every8(ym, 1, 0)),
        pack_y(every8(zm, 3, 0)),
    )
    for n, pair in enumerate(packs):
        s1[2 * n] = pair[0]
        s1[2 * n + 1] = pair[1]

    def moved(v, lanes, rows):
        v = pltpu.roll(v, lax.rem(lanes + 256, 128), 1)
        return pltpu.roll(v, lax.rem(rows + 16, 8), 0)

    s1[10] = moved(to_x, 32 * (3 * ox - g_e), 7 * ox - s_e)

    for n in range(5):

        def gather(i, carry):
            out = []
            for p in range(2):
                v = pltpu.roll(zm[n, tile8(256 * p + 8 * i), :], i, 1)
                out.append(jnp.where(kz == i, v, carry[2 * p]))
                out.append(jnp.where(kz == ((i + 31) & 31), v, carry[2 * p + 1]))
            return tuple(out)

        b0, t0, b1, t1 = lax.fori_loop(0, 32, gather, (zero,) * 4)
        t0, t1 = pltpu.roll(t0, 97, 1), pltpu.roll(t1, 97, 1)
        if n < 4:
            s3[2 * n], s3[2 * n + 1], s2[2 * n], s2[2 * n + 1] = b0, b1, t0, t1
        else:
            second = (sub == lax.rem(s_e + 1, 8)) | (sub == lax.rem(s_c + 1, 8))
            for msg, line, lo, hi in ((s3, s8, b0, b1), (s2, s7, t0, t1)):
                both = jnp.where(second, pltpu.roll(hi, 1, 0), lo)
                msg[9] = both
                line[0] = both
    s3[8] = moved(to_x, i_e, 0)
    s2[8] = moved(to_x, i_e - 31, 0)

    s_o, g_o = 7 * gy, 3 * gy
    s4[0] = jnp.where((sub == s_o) & (grp == g_o), moved(own_y, 32 * (g_o - g_e), s_o - s_e), 0.0)
    s4[1] = jnp.where((sub == 7 * gx) & (grp == 3 * gx), moved(own_x, 32 * (3 * gx - g_e), 7 * gx - s_e), 0.0)
    z_e = zm[0, here_e, :]
    i_o = 31 * gx
    s6[0] = jnp.where(kz == 31, pltpu.roll(z_e, 31, 1), 0.0)
    s5[0] = jnp.where(kz == 0, pltpu.roll(z_e, 97, 1), 0.0)
    s6[1] = jnp.where(kz == i_o, moved(own_x, i_o, 0), 0.0)
    s5[1] = jnp.where(kz == i_o, moved(own_x, i_o - 31, 0), 0.0)
    zy = pack_y(every8(zm, 0, 0))
    for h in range(2):
        s8[1 + h] = jnp.where(kz == 31, pltpu.roll(zy[h], 31, 1), 0.0)
        s7[1 + h] = jnp.where(kz == 0, pltpu.roll(zy[h], 97, 1), 0.0)

    count = 3 + 3 * has_up.astype(jnp.int32) + 3 * has_down.astype(jnp.int32)
    pl.semaphore_wait(barrier, count)

    lands = (0, 1, 3, 2, 4, 6, 5, 8, 7)
    copies = [
        pltpu.make_async_remote_copy(
            src_ref=sends[k], dst_ref=gets[lands[k]], send_sem=send_sem.at[k], recv_sem=recv_sem.at[lands[k]],
            device_id=peers[k], device_id_type=MESH,
        )
        for k in range(9)
    ]
    for k in range(9):
        guarded(k, copies[k].start)

    def arrival(k):
        return pltpu.make_async_remote_copy(
            src_ref=sends[lands[k]], dst_ref=gets[k], send_sem=send_sem.at[k], recv_sem=recv_sem.at[k],
            device_id=peers[k], device_id_type=MESH,
        )

    for k in range(9):
        guarded(k, lambda k=k: arrival(k).wait_recv())

    hi_y, lo_y = oy.astype(F32), gy.astype(F32)
    hi_x, lo_x = ox.astype(F32), gx.astype(F32)
    mid_y = []
    for h in range(2):
        m = r1[4 + h] + r1[6 + h] * s1[h] + r1[8 + h] * (r7[1 + h] + r8[1 + h])
        mid_y.append(m + (hi_x if h == 1 else lo_x) * (r1[10] * r4[1]))
    for n, pair in enumerate(((r1[0], r1[1]), (r1[2], r1[3]), mid_y)):
        for h in range(2):
            for g in range(4):
                rows = pl.ds(32 * h + 8 * g, 8)
                yh[n, rows, :] = hi_y * pltpu.roll(pair[h], (32 * (3 - g)) % 128, 1)
                yh[3 + n, rows, :] = lo_y * pltpu.roll(pair[h], (32 * (0 - g)) % 128, 1)
    corner = (sub == s_e) & (grp == g_e)
    for base, msg, line, cross, own in ((0, r2, r7, r5, s2), (6, r3, r8, r6, s3)):
        for v in range(2):
            side = hi_x if v == 1 else lo_x
            m = msg[4 + v] + msg[6 + v] * own[v] + side * (msg[8] * cross[1])
            c = jnp.broadcast_to(msg[9, pl.ds(lax.rem(s_c + v, 8), 1), :], (8, 128))
            f = jnp.broadcast_to(line[0, pl.ds(lax.rem(s_o + v, 8), 1), :], (8, 128))
            f = pltpu.roll(f, lax.rem(32 * (g_e - g_o) + 128, 128), 1)
            zh[base + v] = msg[v]
            zh[base + 2 + v] = msg[2 + v]
            zh[base + 4 + v] = m + jnp.where(corner, c * f, 0.0)
    mid_x = r0[2] + r0[3] * s0[0] + r0[4] * r4[0] + r0[5] * (r5[0] + r6[0])
    xh[0] = hi_x * mid_x
    xh[1] = lo_x * mid_x
    tf[1, pl.ds(16 * 33 + 1, 8, stride=2), :] = hi_x * r0[0]
    tf[2, pl.ds(0, 8, stride=2), :] = lo_x * r0[0]
    po[2, ROWS + 8 : ROWS + 16, :] = hi_x * r0[1]
    po[1, 0:8, :] = lo_x * r0[1]
    for k in range(9):
        guarded(k, copies[k].wait_send)


CHUNKS = 4


def finish(tf, tg, po, co, yh, zh, xh, out_h, grad_h, mid, term, out, grad, out_sem, grad_sem):
    kz, grp, sub = masks()

    def row(n, x):
        return jnp.broadcast_to(yh[n, pl.ds(x, 1), :], (8, 128))

    def above(n, p, i):
        return pltpu.roll(zh[2 * n + p], 31 - i, 1)

    def below(n, p, i):
        return pltpu.roll(zh[6 + 2 * n + p], lax.rem(128 - i, 128), 1)

    mid[1, ROWS + 8 : ROWS + 16, :] = xh[0]
    mid[2, 0:8, :] = xh[1]

    def middle(i, p):
        x = 32 * p + i
        near = [tf[n, pl.ds(16 * (i + 1) + p, 8, stride=2), :] for n in (0, 3, 4, 5, 6)]
        q = [
            near[0],
            tf[1, pl.ds(16 * (i + 2) + p, 8, stride=2), :],
            tf[2, pl.ds(16 * i + p, 8, stride=2), :],
            y_up(near[1], row(0, x), grp, sub),
            y_down(near[2], row(3, x), grp, sub),
            z_up(near[3], above(0, p, i), kz),
            z_down(near[4], below(0, p, i), kz),
        ]
        here = tile8(8 * x)
        padded = tile8(8 * x + 8)
        ar, b = co[0, here, :], co[1, here, :]
        s = weighted(q, [co[n, here, :] for n in (2, 3, 4)])
        ars = ar * s
        for n in range(7):
            mid[n, padded, :] = ars + b * q[n]
        g = [
            po[0, padded, :],
            po[1, here, :],
            po[2, tile8(8 * x + 16), :],
            y_down(po[3, padded, :], row(4, x), grp, sub),
            y_up(po[4, padded, :], row(1, x), grp, sub),
            z_down(po[5, padded, :], below(1, p, i), kz),
            z_up(po[6, padded, :], above(1, p, i), kz),
        ]
        t = (s - q[0]) * g[0]
        for n in range(1, 7):
            t = t + (s - q[n]) * g[n]
        term[here, :] = t

    def sweep(i, carry):
        middle(i, 0)
        middle(i, 1)
        return carry

    lax.fori_loop(0, 32, sweep, 0)

    def first(i, p):
        x = 32 * p + i
        here = tile8(8 * x)
        padded = tile8(8 * x + 8)
        q = [
            mid[0, padded, :],
            mid[1, tile8(8 * x + 16), :],
            mid[2, here, :],
            y_up(mid[3, padded, :], row(2, x), grp, sub),
            y_down(mid[4, padded, :], row(5, x), grp, sub),
            z_up(mid[5, padded, :], above(2, p, i), kz),
            z_down(mid[6, padded, :], below(2, p, i), kz),
        ]
        ar, b = co[0, here, :], co[1, here, :]
        s = weighted(q, [co[n, here, :] for n in (2, 3, 4)])
        ars = ar * s
        at = tile8(8 * i)
        t = term[here, :]
        for n in range(7):
            out[n, p, at, :] = ars + b * q[n]
            t = t + (s - q[n]) * tg[n, pl.ds(16 * i + p, 8, stride=2), :]
        grad[p, at, :] = co[5, here, :] * t

    def last(i, carry):
        first(i, 0)
        first(i, 1)
        return carry

    copies = []
    step = 32 // CHUNKS
    for c in range(CHUNKS):
        lax.fori_loop(c * step, (c + 1) * step, last, 0)
        rows = pl.ds(8 * step * c, 8 * step)
        copies.append(pltpu.make_async_copy(out.at[:, :, rows, :], out_h.at[:, :, rows, :], out_sem.at[c]))
        copies.append(pltpu.make_async_copy(grad.at[:, rows, :], grad_h.at[:, rows, :], grad_sem.at[c]))
        copies[-2].start()
        copies[-1].start()
    for copy in copies:
        copy.wait()


def on_device(nz, populations, adjoint_final, velocity, particle_kappa, solid_label, tile_active):
    def paired(block):
        n = block.shape[0]
        return block.reshape(n, 2, 256, 128).transpose(0, 2, 1, 3).reshape(n, ROWS, 128)

    args = [
        paired(populations), paired(adjoint_final), paired(velocity),
        particle_kappa.reshape(ROWS, 128), solid_label.reshape(ROWS, 128), tile_active.reshape(1, 2),
    ]
    args = [pltpu.with_memory_space_constraint(a, pltpu.HBM) for a in args]
    hbm, vmem = pl.BlockSpec(memory_space=pltpu.HBM), pl.BlockSpec(memory_space=pltpu.VMEM)
    kept = [
        pltpu.VMEM(shape, F32)
        for shape in (
            (7, ROWS + 32, 128), (7, ROWS, 128), (7, ROWS + 16, 128), (6, ROWS, 128),
            (6, LAYERS, 128), (12, 8, 128), (2, 8, 128),
        )
    ]
    messages = [pltpu.VMEM((n, 8, 128), F32) for n in PARTS]
    held = pl.pallas_call(
        functools.partial(exchange, nz),
        out_shape=kept,
        in_specs=[hbm] * 6,
        out_specs=[vmem] * 7,
        scratch_shapes=[
            pltpu.VMEM((7, ROWS, 128), jnp.bfloat16),
            pltpu.VMEM((7, ROWS, 128), jnp.bfloat16),
            pltpu.VMEM((3, ROWS, 128), jnp.bfloat16),
            pltpu.VMEM((ROWS, 128), F32),
            pltpu.VMEM((ROWS, 128), jnp.int32),
            pltpu.SMEM((1, 2), jnp.int32),
            pltpu.VMEM((3, ROWS, 128), F32),
            pltpu.VMEM((5, ROWS, 128), F32),
            pltpu.VMEM((2, ROWS, 128), F32),
            pltpu.VMEM((4, 8, 128), F32),
            *messages,
            *messages,
            pltpu.SemaphoreType.DMA((6,)),
            pltpu.SemaphoreType.DMA((9,)),
            pltpu.SemaphoreType.DMA((9,)),
        ],
        compiler_params=pltpu.CompilerParams(
            collective_id=0, has_side_effects=True, vmem_limit_bytes=24 * 2**20
        ),
        name="exchange",
    )(*args)
    first, gradient = pl.pallas_call(
        finish,
        out_shape=[
            jax.ShapeDtypeStruct((7, 2, 256, 128), F32),
            jax.ShapeDtypeStruct((2, 256, 128), F32),
        ],
        in_specs=[vmem] * 7,
        out_specs=[hbm] * 2,
        scratch_shapes=[
            pltpu.VMEM((7, ROWS + 16, 128), F32),
            pltpu.VMEM((ROWS, 128), F32),
            pltpu.VMEM((7, 2, 256, 128), F32),
            pltpu.VMEM((2, 256, 128), F32),
            pltpu.SemaphoreType.DMA((CHUNKS,)),
            pltpu.SemaphoreType.DMA((CHUNKS,)),
        ],
        compiler_params=pltpu.CompilerParams(vmem_limit_bytes=24 * 2**20),
        name="finish",
    )(*held)
    voxels = EDGE * EDGE * EDGE
    return first.reshape(7, 2, 1, 1, voxels), gradient.reshape(2, 1, 1, voxels)


def solution(mesh):
    spec, one = P(None, "gx", "gy", "gz", None), P("gx", "gy", "gz", None)
    return jax.shard_map(
        functools.partial(on_device, mesh.shape["gz"]),
        mesh=mesh,
        in_specs=(spec, spec, spec, one, one, P("gx", "gy", "gz")),
        out_specs=(spec, one),
        check_vma=False,
    )
```

```python
import functools

import jax
import jax.numpy as jnp
from jax import lax
from jax.experimental import pallas as pl
from jax.experimental.pallas import tpu as pltpu
from jax.sharding import PartitionSpec as P

EDGE = 32
FLUID_KAPPA = 1.0 / 6.0
MESH = pl.DeviceIdType.MESH
F32 = jnp.float32
LAYERS = 2 * EDGE
ROWS = 8 * LAYERS
PARTS = (6, 11, 10, 10, 2, 2, 2, 3, 3)


def masks():
    lane = lax.broadcasted_iota(jnp.int32, (8, 128), 1)
    sub = lax.broadcasted_iota(jnp.int32, (8, 128), 0)
    return lane & 31, lane >> 5, sub


def pick(flag, yes, no):
    return jnp.where(jnp.broadcast_to(flag, (8, 128)), yes, no)


def z_up(v, halo, kz):
    return jnp.where(kz == 31, halo, pltpu.roll(v, 127, 1))


def z_down(v, halo, kz):
    return jnp.where(kz == 0, halo, pltpu.roll(v, 1, 1))


def y_up(v, halo, grp, sub):
    r = pltpu.roll(v, 96, 1)
    inner = jnp.where(grp == 3, pltpu.roll(r, 7, 0), r)
    return jnp.where((grp == 3) & (sub == 7), halo, inner)


def y_down(v, halo, grp, sub):
    r = pltpu.roll(v, 32, 1)
    inner = jnp.where(grp == 0, pltpu.roll(r, 1, 0), r)
    return jnp.where((grp == 0) & (sub == 0), halo, inner)


def weighted(q, d):
    even = (q[1] + q[2]) + (q[3] + q[4]) + (q[5] + q[6])
    odd = d[0] * (q[1] - q[2]) + d[1] * (q[3] - q[4]) + d[2] * (q[5] - q[6])
    return 0.25 * q[0] + 0.125 * even + 0.5 * odd


def tile8(row):
    return pl.ds(pl.multiple_of(row, 8), 8)


def exchange(
    nz, pop_h, fin_h, vel_h, kap_h, sol_h, act_h,
    tf, tg, po, co, yh, zh, xh,
    popb, finb, velb, kapb, solb, actb, tv, zm, ym, zp,
    s0, s1, s2, s3, s4, s5, s6, s7, s8, r0, r1, r2, r3, r4, r5, r6, r7, r8,
    load_sem, send_sem, recv_sem,
):
    sends = (s0, s1, s2, s3, s4, s5, s6, s7, s8)
    gets = (r0, r1, r2, r3, r4, r5, r6, r7, r8)
    gx, gy, gz = lax.axis_index("gx"), lax.axis_index("gy"), lax.axis_index("gz")
    ox, oy, up, down = 1 - gx, 1 - gy, gz + 1, gz - 1
    peers = (
        (ox, gy, gz), (gx, oy, gz), (gx, gy, up), (gx, gy, down), (ox, oy, gz),
        (ox, gy, up), (ox, gy, down), (gx, oy, up), (gx, oy, down),
    )
    has_up, has_down = gz < nz - 1, gz > 0
    exists = (None, None, has_up, has_down, None, has_up, has_down, has_up, has_down)

    def guarded(k, act):
        if exists[k] is None:
            act()
        else:
            pl.when(exists[k])(act)

    barrier = pltpu.get_barrier_semaphore()
    for k in range(9):
        guarded(k, lambda k=k: pl.semaphore_signal(barrier, inc=1, device_id=peers[k], device_id_type=MESH))
    loads = [
        pltpu.make_async_copy(src, dst, load_sem.at[n])
        for n, (src, dst) in enumerate(
            ((act_h, actb), (fin_h, finb), (vel_h, velb), (kap_h, kapb), (sol_h, solb), (pop_h, popb))
        )
    ]
    for copy in loads:
        copy.start()

    kz, grp, sub = masks()
    zero = jnp.zeros((8, 128), F32)
    s_e, g_e = 7 * oy, 3 * oy
    s_c = lax.rem(s_e + 4, 8)
    i_e, p_e = 31 * ox, ox
    sgx, sgy = (1 - 2 * gx).astype(F32), (1 - 2 * gy).astype(F32)
    first_x, first_y = gx == 0, gy == 0
    fx, fy, bx, by = 1 + ox, 3 + oy, 1 + gx, 3 + gy
    zsign = jnp.where(kz == 0, -0.5, 0.5)

    @pl.when(gz == nz - 1)
    def _():
        for k in (2, 5, 7):
            gets[k][...] = jnp.zeros_like(gets[k])

    @pl.when(gz == 0)
    def _():
        for k in (3, 6, 8):
            gets[k][...] = jnp.zeros_like(gets[k])

    loads[1].wait()
    for n in range(7):
        tf[n, 16 : 16 + ROWS, :] = finb[n].astype(F32)
    for n in (1, 2):
        tf[n, pl.ds(0, 8, stride=2), :] = zero
        tf[n, pl.ds(1, 8, stride=2), :] = tf[n, pl.ds(16 * 32, 8, stride=2), :]
        tf[n, pl.ds(16 * 33, 8, stride=2), :] = tf[n, pl.ds(16 + 1, 8, stride=2), :]
        tf[n, pl.ds(16 * 33 + 1, 8, stride=2), :] = zero
        po[n, 0:8, :] = zero
        po[n, ROWS + 8 : ROWS + 16, :] = zero
    loads[2].wait()
    for n in range(3):
        tv[n] = velb[n].astype(F32)
    loads[5].wait()
    for n in range(7):
        tg[n] = popb[n].astype(F32)
    loads[0].wait()
    loads[3].wait()
    loads[4].wait()
    active = (actb[0, 0].astype(F32), actb[0, 1].astype(F32))

    def cell(i, p, a):
        near = [tf[n, pl.ds(16 * (i + 1) + p, 8, stride=2), :] for n in (0, 3, 4, 5, 6)]
        q = [
            near[0],
            tf[1, pl.ds(16 * (i + 2) + p, 8, stride=2), :],
            tf[2, pl.ds(16 * i + p, 8, stride=2), :],
            y_up(near[1], zero, grp, sub),
            y_down(near[2], zero, grp, sub),
            z_up(near[3], zero, kz),
            z_down(near[4], zero, kz),
        ]
        here = tile8(256 * p + 8 * i)
        solid = solb[here, :] > 0
        kappa = jnp.where(solid, kapb[here, :], FLUID_KAPPA)
        rate = 1.0 / (4.0 * kappa + 0.5)
        ar = a * rate
        b = a - ar
        d = [jnp.where(solid, 0.0, tv[n, pl.ds(16 * i + p, 8, stride=2), :]) for n in range(3)]
        return near, q, solid, rate, ar, b, d, ar * weighted(q, d)

    def layer(i, p):
        x = 32 * p + i
        near, q, solid, rate, ar, b, d, ars = cell(i, p, active[p])
        here = tile8(8 * x)
        padded = tile8(8 * x + 8)
        for n, c in enumerate((ar, b, d[0], d[1], d[2])):
            co[n, here, :] = c
        co[5, here, :] = jnp.where(solid, -4.0 * active[p] * rate * rate, 0.0)
        g = [tg[n, pl.ds(16 * i + p, 8, stride=2), :] for n in range(7)]
        total = ((g[0] + g[1]) + (g[2] + g[3])) + ((g[4] + g[5]) + g[6])
        w = ar * total
        post = [b * g[0] + 0.25 * w]
        for n in range(3):
            even, odd = 0.125 * w, 0.5 * (w * d[n])
            post.append(b * g[2 * n + 1] + (even + odd))
            post.append(b * g[2 * n + 2] + (even - odd))
        for n in range(7):
            po[n, padded, :] = post[n]
        to_y = ar * (0.125 + 0.5 * sgy * d[1])
        bottom = kz == 0
        zm[0, here, :] = jnp.where(bottom, near[3], near[4])
        zm[1, here, :] = jnp.where(bottom, post[6], post[5])
        zm[2, here, :] = ars + b * jnp.where(bottom, q[5], q[6])
        zm[3, here, :] = ar * (0.125 + zsign * d[2])
        zm[4, here, :] = jnp.where(sub == s_e, pick(first_y, near[2], near[1]), pltpu.roll(to_y, 4, 0))
        ym[0, here, :] = ars + b * pick(first_y, q[4], q[3])
        ym[1, here, :] = to_y

    def sweep(i, carry):
        layer(i, 0)
        layer(i, 1)
        return carry

    lax.fori_loop(0, 32, sweep, 0, unroll=8)

    a_e = jnp.where(first_x, active[1], active[0])
    near, q, solid, rate, ar, b, d, ars = cell(i_e, p_e, a_e)
    x_e = 63 * ox
    here_e = tile8(8 * x_e)
    to_x = ar * (0.125 + 0.5 * sgx * d[0])
    own_x = tf[fx, pl.ds(16 * (i_e + 1) + p_e, 8, stride=2), :]
    own_y = pick(first_y, near[2], near[1])
    s0[0] = own_x
    s0[1] = po[bx, tile8(8 * x_e + 8), :]
    s0[2] = ars + b * pick(first_x, q[2], q[1])
    s0[3] = to_x
    s0[4] = ym[1, here_e, :]
    s0[5] = zm[3, here_e, :]

    def pack_y(read):
        out = []
        for h in range(2):
            v = zero
            for g in range(4):
                rows = read(32 * h + 8 * g, h, 8 * g)
                v = jnp.where(grp == g, pltpu.roll(rows, lax.rem(32 * (g - g_e) + 128, 128), 1), v)
            out.append(v)
        return out

    def every8(ref, n, pad):
        return lambda x, h, i: ref[n, pl.ds(8 * (x + pad) + s_e, 8, stride=8), :]

    packs = (
        pack_y(lambda x, h, i: tf[fy, pl.ds(16 * (i + 1) + h + 2 * s_e, 8, stride=16), :]),
        pack_y(every8(po, by, 1)),
        pack_y(every8(ym, 0, 0)),
        pack_y(every8(ym, 1, 0)),
        pack_y(every8(zm, 3, 0)),
    )
    for n, pair in enumerate(packs):
        s1[2 * n] = pair[0]
        s1[2 * n + 1] = pair[1]

    def moved(v, lanes, rows):
        v = pltpu.roll(v, lax.rem(lanes + 256, 128), 1)
        return pltpu.roll(v, lax.rem(rows + 16, 8), 0)

    s1[10] = moved(to_x, 32 * (3 * ox - g_e), 7 * ox - s_e)

    for n in range(5):

        b0, t0, b1, t1 = (zero,) * 4
        for i in range(32):
            v0 = pltpu.roll(zm[n, 8 * i : 8 * i + 8, :], i, 1)
            v1 = pltpu.roll(zm[n, 256 + 8 * i : 264 + 8 * i, :], i, 1)
            bottom, top = kz == i, kz == (i + 31) % 32
            b0, t0 = jnp.where(bottom, v0, b0), jnp.where(top, v0, t0)
            b1, t1 = jnp.where(bottom, v1, b1), jnp.where(top, v1, t1)
        t0, t1 = pltpu.roll(t0, 97, 1), pltpu.roll(t1, 97, 1)
        if n < 4:
            s3[2 * n], s3[2 * n + 1], s2[2 * n], s2[2 * n + 1] = b0, b1, t0, t1
        else:
            second = (sub == lax.rem(s_e + 1, 8)) | (sub == lax.rem(s_c + 1, 8))
            for msg, line, lo, hi in ((s3, s8, b0, b1), (s2, s7, t0, t1)):
                both = jnp.where(second, pltpu.roll(hi, 1, 0), lo)
                msg[9] = both
                line[0] = both
    s3[8] = moved(to_x, i_e, 0)
    s2[8] = moved(to_x, i_e - 31, 0)

    s_o, g_o = 7 * gy, 3 * gy
    s4[0] = jnp.where((sub == s_o) & (grp == g_o), moved(own_y, 32 * (g_o - g_e), s_o - s_e), 0.0)
    s4[1] = jnp.where((sub == 7 * gx) & (grp == 3 * gx), moved(own_x, 32 * (3 * gx - g_e), 7 * gx - s_e), 0.0)
    z_e = zm[0, here_e, :]
    i_o = 31 * gx
    s6[0] = jnp.where(kz == 31, pltpu.roll(z_e, 31, 1), 0.0)
    s5[0] = jnp.where(kz == 0, pltpu.roll(z_e, 97, 1), 0.0)
    s6[1] = jnp.where(kz == i_o, moved(own_x, i_o, 0), 0.0)
    s5[1] = jnp.where(kz == i_o, moved(own_x, i_o - 31, 0), 0.0)
    zy = pack_y(every8(zm, 0, 0))
    for h in range(2):
        s8[1 + h] = jnp.where(kz == 31, pltpu.roll(zy[h], 31, 1), 0.0)
        s7[1 + h] = jnp.where(kz == 0, pltpu.roll(zy[h], 97, 1), 0.0)

    count = 3 + 3 * has_up.astype(jnp.int32) + 3 * has_down.astype(jnp.int32)
    pl.semaphore_wait(barrier, count)

    lands = (0, 1, 3, 2, 4, 6, 5, 8, 7)
    copies = [
        pltpu.make_async_remote_copy(
            src_ref=sends[k], dst_ref=gets[lands[k]], send_sem=send_sem.at[k], recv_sem=recv_sem.at[lands[k]],
            device_id=peers[k], device_id_type=MESH,
        )
        for k in range(9)
    ]
    for k in range(9):
        guarded(k, copies[k].start)

    def arrival(k):
        return pltpu.make_async_remote_copy(
            src_ref=sends[lands[k]], dst_ref=gets[k], send_sem=send_sem.at[k], recv_sem=recv_sem.at[k],
            device_id=peers[k], device_id_type=MESH,
        )

    for k in range(9):
        guarded(k, lambda k=k: arrival(k).wait_recv())

    hi_y, lo_y = oy.astype(F32), gy.astype(F32)
    hi_x, lo_x = ox.astype(F32), gx.astype(F32)
    mid_y = []
    for h in range(2):
        m = r1[4 + h] + r1[6 + h] * s1[h] + r1[8 + h] * (r7[1 + h] + r8[1 + h])
        mid_y.append(m + (hi_x if h == 1 else lo_x) * (r1[10] * r4[1]))
    for n, pair in enumerate(((r1[0], r1[1]), (r1[2], r1[3]), mid_y)):
        for h in range(2):
            for g in range(4):
                rows = pl.ds(32 * h + 8 * g, 8)
                yh[n, rows, :] = hi_y * pltpu.roll(pair[h], (32 * (3 - g)) % 128, 1)
                yh[3 + n, rows, :] = lo_y * pltpu.roll(pair[h], (32 * (0 - g)) % 128, 1)
    corner = (sub == s_e) & (grp == g_e)
    for base, msg, line, cross, own in ((0, r2, r7, r5, s2), (6, r3, r8, r6, s3)):
        for v in range(2):
            side = hi_x if v == 1 else lo_x
            m = msg[4 + v] + msg[6 + v] * own[v] + side * (msg[8] * cross[1])
            c = jnp.broadcast_to(msg[9, pl.ds(lax.rem(s_c + v, 8), 1), :], (8, 128))
            f = jnp.broadcast_to(line[0, pl.ds(lax.rem(s_o + v, 8), 1), :], (8, 128))
            f = pltpu.roll(f, lax.rem(32 * (g_e - g_o) + 128, 128), 1)
            zh[base + v] = msg[v]
            zh[base + 2 + v] = msg[2 + v]
            zh[base + 4 + v] = m + jnp.where(corner, c * f, 0.0)
    mid_x = r0[2] + r0[3] * s0[0] + r0[4] * r4[0] + r0[5] * (r5[0] + r6[0])
    xh[0] = hi_x * mid_x
    xh[1] = lo_x * mid_x
    tf[1, pl.ds(16 * 33 + 1, 8, stride=2), :] = hi_x * r0[0]
    tf[2, pl.ds(0, 8, stride=2), :] = lo_x * r0[0]
    po[2, ROWS + 8 : ROWS + 16, :] = hi_x * r0[1]
    po[1, 0:8, :] = lo_x * r0[1]
    for k in range(9):
        guarded(k, copies[k].wait_send)


CHUNKS = 4


def finish(tf, tg, po, co, yh, zh, xh, out_h, grad_h, mid, term, out, grad, out_sem, grad_sem):
    kz, grp, sub = masks()

    def row(n, x):
        return jnp.broadcast_to(yh[n, pl.ds(x, 1), :], (8, 128))

    def above(n, p, i):
        return pltpu.roll(zh[2 * n + p], 31 - i, 1)

    def below(n, p, i):
        return pltpu.roll(zh[6 + 2 * n + p], lax.rem(128 - i, 128), 1)

    mid[1, ROWS + 8 : ROWS + 16, :] = xh[0]
    mid[2, 0:8, :] = xh[1]

    def middle(i, p):
        x = 32 * p + i
        near = [tf[n, pl.ds(16 * (i + 1) + p, 8, stride=2), :] for n in (0, 3, 4, 5, 6)]
        q = [
            near[0],
            tf[1, pl.ds(16 * (i + 2) + p, 8, stride=2), :],
            tf[2, pl.ds(16 * i + p, 8, stride=2), :],
            y_up(near[1], row(0, x), grp, sub),
            y_down(near[2], row(3, x), grp, sub),
            z_up(near[3], above(0, p, i), kz),
            z_down(near[4], below(0, p, i), kz),
        ]
        here = tile8(8 * x)
        padded = tile8(8 * x + 8)
        ar, b = co[0, here, :], co[1, here, :]
        s = weighted(q, [co[n, here, :] for n in (2, 3, 4)])
        ars = ar * s
        for n in range(7):
            mid[n, padded, :] = ars + b * q[n]
        g = [
            po[0, padded, :],
            po[1, here, :],
            po[2, tile8(8 * x + 16), :],
            y_down(po[3, padded, :], row(4, x), grp, sub),
            y_up(po[4, padded, :], row(1, x), grp, sub),
            z_down(po[5, padded, :], below(1, p, i), kz),
            z_up(po[6, padded, :], above(1, p, i), kz),
        ]
        t = (s - q[0]) * g[0]
        for n in range(1, 7):
            t = t + (s - q[n]) * g[n]
        term[here, :] = t

    def sweep(i, carry):
        middle(i, 0)
        middle(i, 1)
        return carry

    lax.fori_loop(0, 32, sweep, 0, unroll=8)

    def first(i, p):
        x = 32 * p + i
        here = tile8(8 * x)
        padded = tile8(8 * x + 8)
        q = [
            mid[0, padded, :],
            mid[1, tile8(8 * x + 16), :],
            mid[2, here, :],
            y_up(mid[3, padded, :], row(2, x), grp, sub),
            y_down(mid[4, padded, :], row(5, x), grp, sub),
            z_up(mid[5, padded, :], above(2, p, i), kz),
            z_down(mid[6, padded, :], below(2, p, i), kz),
        ]
        ar, b = co[0, here, :], co[1, here, :]
        s = weighted(q, [co[n, here, :] for n in (2, 3, 4)])
        ars = ar * s
        at = tile8(8 * i)
        t = term[here, :]
        for n in range(7):
            out[n, p, at, :] = ars + b * q[n]
            t = t + (s - q[n]) * tg[n, pl.ds(16 * i + p, 8, stride=2), :]
        grad[p, at, :] = co[5, here, :] * t

    def last(i, carry):
        first(i, 0)
        first(i, 1)
        return carry

    copies = []
    step = 32 // CHUNKS
    for c in range(CHUNKS):
        lax.fori_loop(c * step, (c + 1) * step, last, 0, unroll=8)
        rows = pl.ds(8 * step * c, 8 * step)
        copies.append(pltpu.make_async_copy(out.at[:, :, rows, :], out_h.at[:, :, rows, :], out_sem.at[c]))
        copies.append(pltpu.make_async_copy(grad.at[:, rows, :], grad_h.at[:, rows, :], grad_sem.at[c]))
        copies[-2].start()
        copies[-1].start()
    for copy in copies:
        copy.wait()


def on_device(nz, populations, adjoint_final, velocity, particle_kappa, solid_label, tile_active):
    def paired(block):
        n = block.shape[0]
        return block.reshape(n, 2, 256, 128).transpose(0, 2, 1, 3).reshape(n, ROWS, 128)

    args = [
        paired(populations), paired(adjoint_final), paired(velocity),
        particle_kappa.reshape(ROWS, 128), solid_label.reshape(ROWS, 128), tile_active.reshape(1, 2),
    ]
    args = [pltpu.with_memory_space_constraint(a, pltpu.HBM) for a in args]
    hbm, vmem = pl.BlockSpec(memory_space=pltpu.HBM), pl.BlockSpec(memory_space=pltpu.VMEM)
    kept = [
        pltpu.VMEM(shape, F32)
        for shape in (
            (7, ROWS + 32, 128), (7, ROWS, 128), (7, ROWS + 16, 128), (6, ROWS, 128),
            (6, LAYERS, 128), (12, 8, 128), (2, 8, 128),
        )
    ]
    messages = [pltpu.VMEM((n, 8, 128), F32) for n in PARTS]
    held = pl.pallas_call(
        functools.partial(exchange, nz),
        out_shape=kept,
        in_specs=[hbm] * 6,
        out_specs=[vmem] * 7,
        scratch_shapes=[
            pltpu.VMEM((7, ROWS, 128), jnp.bfloat16),
            pltpu.VMEM((7, ROWS, 128), jnp.bfloat16),
            pltpu.VMEM((3, ROWS, 128), jnp.bfloat16),
            pltpu.VMEM((ROWS, 128), F32),
            pltpu.VMEM((ROWS, 128), jnp.int32),
            pltpu.SMEM((1, 2), jnp.int32),
            pltpu.VMEM((3, ROWS, 128), F32),
            pltpu.VMEM((5, ROWS, 128), F32),
            pltpu.VMEM((2, ROWS, 128), F32),
            pltpu.VMEM((4, 8, 128), F32),
            *messages,
            *messages,
            pltpu.SemaphoreType.DMA((6,)),
            pltpu.SemaphoreType.DMA((9,)),
            pltpu.SemaphoreType.DMA((9,)),
        ],
        compiler_params=pltpu.CompilerParams(
            collective_id=0, has_side_effects=True, vmem_limit_bytes=24 * 2**20
        ),
        name="exchange",
    )(*args)
    first, gradient = pl.pallas_call(
        finish,
        out_shape=[
            jax.ShapeDtypeStruct((7, 2, 256, 128), F32),
            jax.ShapeDtypeStruct((2, 256, 128), F32),
        ],
        in_specs=[vmem] * 7,
        out_specs=[hbm] * 2,
        scratch_shapes=[
            pltpu.VMEM((7, ROWS + 16, 128), F32),
            pltpu.VMEM((ROWS, 128), F32),
            pltpu.VMEM((7, 2, 256, 128), F32),
            pltpu.VMEM((2, 256, 128), F32),
            pltpu.SemaphoreType.DMA((CHUNKS,)),
            pltpu.SemaphoreType.DMA((CHUNKS,)),
        ],
        compiler_params=pltpu.CompilerParams(vmem_limit_bytes=24 * 2**20),
        name="finish",
    )(*held)
    voxels = EDGE * EDGE * EDGE
    return first.reshape(7, 2, 1, 1, voxels), gradient.reshape(2, 1, 1, voxels)


def solution(mesh):
    spec, one = P(None, "gx", "gy", "gz", None), P("gx", "gy", "gz", None)
    return jax.shard_map(
        functools.partial(on_device, mesh.shape["gz"]),
        mesh=mesh,
        in_specs=(spec, spec, spec, one, one, P("gx", "gy", "gz")),
        out_specs=(spec, one),
        check_vma=False,
    )
```

```python
import functools

import jax
import jax.numpy as jnp
from jax import lax
from jax.experimental import pallas as pl
from jax.experimental.pallas import tpu as pltpu
from jax.sharding import PartitionSpec as P

EDGE = 32
FLUID_KAPPA = 1.0 / 6.0
MESH = pl.DeviceIdType.MESH
F32 = jnp.float32
LAYERS = 2 * EDGE
ROWS = 8 * LAYERS
PARTS = (48, 73, 74, 74, 2, 8, 8, 10, 10)


def masks():
    lane = lax.broadcasted_iota(jnp.int32, (8, 128), 1)
    sub = lax.broadcasted_iota(jnp.int32, (8, 128), 0)
    return lane & 31, lane >> 5, sub


def pick(flag, yes, no):
    return jnp.where(jnp.broadcast_to(flag, (8, 128)), yes, no)


def z_up(v, halo, kz):
    return jnp.where(kz == 31, halo, pltpu.roll(v, 127, 1))


def z_down(v, halo, kz):
    return jnp.where(kz == 0, halo, pltpu.roll(v, 1, 1))


def y_up(v, after, halo, grp, sub):
    return pltpu.roll(jnp.where(grp == 0, jnp.where(sub == 7, halo, after), v), 96, 1)


def y_down(v, before, halo, grp, sub):
    return pltpu.roll(jnp.where(grp == 3, jnp.where(sub == 0, halo, before), v), 32, 1)


def weighted(q, d):
    even = (q[1] + q[2]) + (q[3] + q[4]) + (q[5] + q[6])
    odd = d[0] * (q[1] - q[2]) + d[1] * (q[3] - q[4]) + d[2] * (q[5] - q[6])
    return 0.25 * q[0] + 0.125 * even + 0.5 * odd


def part(n):
    return slice(8 * n, 8 * n + 8)


def tile8(row):
    return pl.ds(pl.multiple_of(row, 8), 8)


def exchange(
    nz, pop_h, fin_h, vel_h, kap_h, sol_h, act_h,
    tf, tg, po, co, yh, zh, xh,
    popb, finb, velb, kapb, solb, actb, tv, zm, ym, zp,
    s0, s1, s2, s3, s4, s5, s6, s7, s8, r0, r1, r2, r3, r4, r5, r6, r7, r8,
    load_sem, send_sem, recv_sem, ready,
):
    sends = (s0, s1, s2, s3, s4, s5, s6, s7, s8)
    gets = (r0, r1, r2, r3, r4, r5, r6, r7, r8)
    gx, gy, gz = lax.axis_index("gx"), lax.axis_index("gy"), lax.axis_index("gz")
    ox, oy, up, down = 1 - gx, 1 - gy, gz + 1, gz - 1
    peers = (
        (ox, gy, gz), (gx, oy, gz), (gx, gy, up), (gx, gy, down), (ox, oy, gz),
        (ox, gy, up), (ox, gy, down), (gx, oy, up), (gx, oy, down),
    )
    has_up, has_down = gz < nz - 1, gz > 0
    exists = (None, None, has_up, has_down, None, has_up, has_down, has_up, has_down)
    root = (gx == 0) & (gy == 0) & (gz == 0)
    other = jnp.logical_not(root)
    to_root = [(x == 0) & (y == 0) & (z == 0) for x, y, z in peers]

    def guarded(k, act, also=None):
        flag = exists[k]
        if also is not None:
            flag = also if flag is None else flag & also
        if flag is None:
            act()
        else:
            pl.when(flag)(act)

    barrier = pltpu.get_barrier_semaphore()

    def signal(k, semaphore):
        return lambda: pl.semaphore_signal(semaphore, inc=1, device_id=peers[k], device_id_type=MESH)

    for k in range(9):
        guarded(k, signal(k, barrier), other)
    count = 3 + 3 * has_up.astype(jnp.int32) + 3 * has_down.astype(jnp.int32)
    near_root = functools.reduce(jnp.logical_or, to_root)
    loads = [
        pltpu.make_async_copy(src, dst, load_sem.at[n])
        for n, (src, dst) in enumerate(
            ((act_h, actb), (fin_h, finb), (vel_h, velb), (kap_h, kapb), (sol_h, solb), (pop_h, popb))
        )
    ]
    for copy in loads:
        copy.start()

    @pl.when(root)
    def _():
        pl.semaphore_wait(barrier, count)
        for k in range(9):
            guarded(k, signal(k, ready))

    lands = (0, 1, 3, 2, 4, 6, 5, 8, 7)
    copies = [
        pltpu.make_async_remote_copy(
            src_ref=sends[k], dst_ref=gets[lands[k]], send_sem=send_sem.at[k], recv_sem=recv_sem.at[lands[k]],
            device_id=peers[k], device_id_type=MESH,
        )
        for k in range(9)
    ]

    kz, grp, sub = masks()
    zero = jnp.zeros((8, 128), F32)
    s_e, g_e = 7 * oy, 3 * oy
    s_c = lax.rem(s_e + 4, 8)
    i_e, p_e = 31 * ox, ox
    sgx, sgy = (1 - 2 * gx).astype(F32), (1 - 2 * gy).astype(F32)
    first_x, first_y = gx == 0, gy == 0
    fx, fy, bx, by = 1 + ox, 3 + oy, 1 + gx, 3 + gy
    zsign = jnp.where(kz == 0, -0.5, 0.5)

    @pl.when(gz == nz - 1)
    def _():
        for k in (2, 5, 7):
            gets[k][...] = jnp.zeros_like(gets[k])

    @pl.when(gz == 0)
    def _():
        for k in (3, 6, 8):
            gets[k][...] = jnp.zeros_like(gets[k])

    loads[1].wait()
    for n in range(7):
        tf[n, 16 : 16 + ROWS, :] = finb[n].astype(F32)
    for n in (1, 2):
        tf[n, pl.ds(0, 8, stride=2), :] = zero
        tf[n, pl.ds(1, 8, stride=2), :] = tf[n, pl.ds(16 * 32, 8, stride=2), :]
        tf[n, pl.ds(16 * 33, 8, stride=2), :] = tf[n, pl.ds(16 + 1, 8, stride=2), :]
        tf[n, pl.ds(16 * 33 + 1, 8, stride=2), :] = zero
        po[n, 0:8, :] = zero
        po[n, ROWS + 8 : ROWS + 16, :] = zero
    loads[2].wait()
    for n in range(3):
        tv[n] = velb[n].astype(F32)
    loads[5].wait()
    for n in range(7):
        tg[n] = popb[n].astype(F32)
    loads[0].wait()
    loads[3].wait()
    loads[4].wait()
    active = (actb[0, 0].astype(F32), actb[0, 1].astype(F32))

    def cell(i, p, a):
        near = [tf[n, pl.ds(16 * (i + 1) + p, 8, stride=2), :] for n in (0, 3, 4, 5, 6)]
        q = [
            near[0],
            tf[1, pl.ds(16 * (i + 2) + p, 8, stride=2), :],
            tf[2, pl.ds(16 * i + p, 8, stride=2), :],
            y_up(near[1], tf[3, pl.ds(16 * (i + 1) + p + 2, 8, stride=2), :], zero, grp, sub),
            y_down(near[2], tf[4, pl.ds(16 * (i + 1) + p - 2, 8, stride=2), :], zero, grp, sub),
            z_up(near[3], zero, kz),
            z_down(near[4], zero, kz),
        ]
        here = tile8(256 * p + 8 * i)
        solid = solb[here, :] > 0
        kappa = jnp.where(solid, kapb[here, :], FLUID_KAPPA)
        rate = 1.0 / (4.0 * kappa + 0.5)
        ar = a * rate
        b = a - ar
        d = [jnp.where(solid, 0.0, tv[n, pl.ds(16 * i + p, 8, stride=2), :]) for n in range(3)]
        return near, q, solid, rate, ar, b, d, ar * weighted(q, d)

    def layer(i, p, a):
        x = 32 * p + i
        near, q, solid, rate, ar, b, d, ars = cell(i, p, a)
        here = tile8(8 * x)
        padded = tile8(8 * x + 8)
        for n, c in enumerate((ar, b, d[0], d[1], d[2])):
            co[n, here, :] = c
        co[5, here, :] = jnp.where(solid, -4.0 * a * rate * rate, 0.0)
        g = [tg[n, pl.ds(16 * i + p, 8, stride=2), :] for n in range(7)]
        total = ((g[0] + g[1]) + (g[2] + g[3])) + ((g[4] + g[5]) + g[6])
        w = ar * total
        post = [b * g[0] + 0.25 * w]
        for n in range(3):
            even, odd = 0.125 * w, 0.5 * (w * d[n])
            post.append(b * g[2 * n + 1] + (even + odd))
            post.append(b * g[2 * n + 2] + (even - odd))
        for n in range(7):
            po[n, padded, :] = post[n]
        to_y = ar * (0.125 + 0.5 * sgy * d[1])
        bottom = kz == 0
        zm[0, here, :] = jnp.where(bottom, near[3], near[4])
        zm[1, here, :] = jnp.where(bottom, post[6], post[5])
        zm[2, here, :] = ars + b * jnp.where(bottom, q[5], q[6])
        zm[3, here, :] = ar * (0.125 + zsign * d[2])
        zm[4, here, :] = jnp.where(sub == s_e, pick(first_y, near[2], near[1]), pltpu.roll(to_y, 4, 0))
        ym[0, here, :] = ars + b * pick(first_y, q[4], q[3])
        ym[1, here, :] = to_y
        return near, q, ar, b, d, ars

    def sweep(i, carry):
        layer(i, 0, active[0])
        layer(i, 1, active[1])
        return carry

    a_e = jnp.where(first_x, active[1], active[0])
    near, q, ar, b, d, ars = layer(i_e, p_e, a_e)
    x_e = 63 * ox
    here_e = tile8(8 * x_e)
    to_x = ar * (0.125 + 0.5 * sgx * d[0])
    own_x = tf[fx, pl.ds(16 * (i_e + 1) + p_e, 8, stride=2), :]
    own_y = pick(first_y, near[2], near[1])
    s0[part(0)] = own_x
    s0[part(1)] = po[bx, tile8(8 * x_e + 8), :]
    s0[part(2)] = ars + b * pick(first_x, q[2], q[1])
    s0[part(3)] = to_x
    s0[part(4)] = ym[1, here_e, :]
    s0[part(5)] = zm[3, here_e, :]
    pl.when(root)(copies[0].start)

    lax.fori_loop(0, 32, sweep, 0, unroll=8)

    def pack_y(read):
        out = []
        for h in range(2):
            v = zero
            for g in range(4):
                rows = read(32 * h + 8 * g, h, 8 * g)
                v = jnp.where(grp == g, pltpu.roll(rows, lax.rem(32 * (g - g_e) + 128, 128), 1), v)
            out.append(v)
        return out

    def every8(ref, n, pad):
        return lambda x, h, i: ref[n, pl.ds(8 * (x + pad) + s_e, 8, stride=8), :]

    packs = (
        pack_y(lambda x, h, i: tf[fy, pl.ds(16 * (i + 1) + h + 2 * s_e, 8, stride=16), :]),
        pack_y(every8(po, by, 1)),
        pack_y(every8(ym, 0, 0)),
        pack_y(every8(ym, 1, 0)),
        pack_y(every8(zm, 3, 0)),
    )
    for n, pair in enumerate(packs[:4]):
        s1[part(2 * n)] = pair[0]
        s1[part(2 * n + 1)] = pair[1]
    s1[part(8)] = jnp.where((kz == 7) | (kz == 8), pltpu.roll(packs[4][1], 8, 1), packs[4][0])

    def shifted(v, lanes):
        return pltpu.roll(v, lax.rem(lanes + 256, 128), 1)

    zp[0] = shifted(to_x, 32 * (3 * ox - g_e))
    s1[72:73, :] = zp[0, pl.ds(s_e, 1), :]

    for n in range(5):

        b0, t0, b1, t1 = (zero,) * 4
        for i in range(32):
            v0 = pltpu.roll(zm[n, 8 * i : 8 * i + 8, :], i, 1)
            v1 = pltpu.roll(zm[n, 256 + 8 * i : 264 + 8 * i, :], i, 1)
            bottom, top = kz == i, kz == (i + 31) % 32
            b0, t0 = jnp.where(bottom, v0, b0), jnp.where(top, v0, t0)
            b1, t1 = jnp.where(bottom, v1, b1), jnp.where(top, v1, t1)
        t0, t1 = pltpu.roll(t0, 97, 1), pltpu.roll(t1, 97, 1)
        if n < 4:
            for msg, v, value in ((s3, 0, b0), (s3, 1, b1), (s2, 0, t0), (s2, 1, t1)):
                msg[part(2 * n + v)] = value
        else:
            for v, line in enumerate((b0, b1, t0, t1)):
                zp[1 + v] = line
            for v, (msg, other_msg) in enumerate(((s3, s8), (s2, s7))):
                for h in range(2):
                    msg[72 + h : 73 + h, :] = zp[1 + 2 * v + h, pl.ds(s_c, 1), :]
                    other_msg[8 + h : 9 + h, :] = zp[1 + 2 * v + h, pl.ds(s_e, 1), :]
    s3[part(8)] = shifted(to_x, i_e)
    s2[part(8)] = shifted(to_x, i_e - 31)

    s_o, g_o = 7 * gy, 3 * gy
    zp[5] = jnp.where(grp == g_o, shifted(own_y, 32 * (g_o - g_e)), 0.0)
    zp[6] = jnp.where(grp == 3 * gx, shifted(own_x, 32 * (3 * gx - g_e)), 0.0)
    s4[0:1, :] = zp[5, pl.ds(s_e, 1), :]
    s4[1:2, :] = zp[6, pl.ds(s_e, 1), :]
    z_e = zm[0, here_e, :]
    s6[...] = jnp.where(kz == 16, pltpu.roll(own_x, 16, 1), pltpu.roll(z_e, 31, 1))
    s5[...] = jnp.where(kz == 16, pltpu.roll(own_x, 113, 1), pltpu.roll(z_e, 97, 1))
    zy = pack_y(every8(zm, 0, 0))
    s8[0:8, :] = jnp.where(kz == 7, pltpu.roll(zy[1], 39, 1), pltpu.roll(zy[0], 31, 1))
    s7[0:8, :] = jnp.where(kz == 8, pltpu.roll(zy[1], 105, 1), pltpu.roll(zy[0], 97, 1))

    order = (4, 5, 6, 7, 8, 1, 2, 3, 0)

    @pl.when(root)
    def _():
        for k in order[:-1]:
            guarded(k, copies[k].start)

    @pl.when(other)
    def _():
        pl.semaphore_wait(barrier, count - near_root.astype(jnp.int32))
        for k in order:
            guarded(k, copies[k].start, jnp.logical_not(to_root[k]))

    @pl.when(near_root)
    def _():
        pl.semaphore_wait(ready, 1)
        for k in order:
            pl.when(to_root[k])(copies[k].start)

    def arrival(k):
        return pltpu.make_async_remote_copy(
            src_ref=sends[lands[k]], dst_ref=gets[k], send_sem=send_sem.at[k], recv_sem=recv_sem.at[k],
            device_id=peers[k], device_id_type=MESH,
        )

    for k in range(9):
        guarded(k, lambda k=k: arrival(k).wait_recv())

    hi_x, lo_x = ox.astype(F32), gx.astype(F32)

    def spread(row):
        return jnp.broadcast_to(row, (8, 128))

    top, bottom = kz == 31, kz == 0
    line_y = jnp.where(sub == 7 * ox, spread(r4[1:2, :]), 0.0)
    mid_y = []
    for h in range(2):
        edge = [r1[part(8)], r7[0:8, :], r8[0:8, :]]
        if h == 1:
            edge = [pltpu.roll(v, 120, 1) for v in edge]
        m = r1[part(4 + h)] + r1[part(6 + h)] * s1[part(h)]
        m = m + edge[0] * (jnp.where(top, edge[1], 0.0) + jnp.where(bottom, edge[2], 0.0))
        mid_y.append(m + (hi_x if h == 1 else lo_x) * (spread(r1[72:73, :]) * line_y))
    for n, pair in enumerate(((r1[part(0)], r1[part(1)]), (r1[part(2)], r1[part(3)]), mid_y)):
        for h in range(2):
            for g in range(4):
                yh[n, pl.ds(32 * h + 8 * g, 8), :] = pltpu.roll(pair[h], lax.rem(32 * (g_o - g) + 128, 128), 1)
    corner = (sub == s_e) & (grp == g_e)
    for base, msg, line, cross, own in ((0, r2, r7, r5, s2), (6, r3, r8, r6, s3)):
        line_z = jnp.where(kz == i_e, shifted(cross[...], i_e - 16), 0.0)
        for v in range(2):
            side = hi_x if v == 1 else lo_x
            m = msg[part(4 + v)] + msg[part(6 + v)] * own[part(v)] + side * (msg[part(8)] * line_z)
            f = shifted(spread(line[8 + v : 9 + v, :]), 32 * (g_e - g_o))
            m = m + jnp.where(corner, spread(msg[72 + v : 73 + v, :]) * f, 0.0)
            for n, halo in enumerate((msg[part(v)], msg[part(2 + v)], m)):
                zh[base + 2 * n + v] = halo if base == 0 else pltpu.roll(halo, 97, 1)
    mid_x = r0[part(2)] + r0[part(3)] * s0[part(0)]
    mid_x = mid_x + r0[part(4)] * jnp.where(sub == s_e, spread(r4[0:1, :]), 0.0)
    mid_x = mid_x + r0[part(5)] * (jnp.where(top, r5[...], 0.0) + jnp.where(bottom, r6[...], 0.0))
    xh[0] = hi_x * mid_x
    xh[1] = lo_x * mid_x
    tf[1, pl.ds(16 * 33 + 1, 8, stride=2), :] = hi_x * r0[part(0)]
    tf[2, pl.ds(0, 8, stride=2), :] = lo_x * r0[part(0)]
    po[2, ROWS + 8 : ROWS + 16, :] = hi_x * r0[part(1)]
    po[1, 0:8, :] = lo_x * r0[part(1)]
    for k in range(9):
        guarded(k, copies[k].wait_send)


BLOCK = 16
CHUNKS = LAYERS // BLOCK


def finish(tf, tg, po, co, yh, zh, xh, out_h, grad_h, mid, term, out, grad, out_sem, grad_sem):
    kz, grp, sub = masks()
    gy = lax.axis_index("gy")
    hi_y, lo_y = (1 - gy).astype(F32), gy.astype(F32)

    def row(n, x):
        r = jnp.broadcast_to(yh[n, x : x + 1, :], (8, 128))
        return hi_y * r, lo_y * r

    def both_z(n, p, i):
        return pltpu.roll(jnp.where(kz == i, zh[2 * n + p], zh[6 + 2 * n + p]), 31 - i, 1)

    mid[1, ROWS + 8 : ROWS + 16, :] = xh[0]
    mid[2, 0:8, :] = xh[1]

    def middle(x):
        p, i = x // 32, x % 32

        def near(n, rows):
            return tf[n, pl.ds(16 * (i + 1) + p + 2 * rows, 8, stride=2), :]

        hi, lo = row(0, x)
        hz = both_z(0, p, i)
        q = [
            near(0, 0),
            near(1, 8),
            near(2, -8),
            y_up(near(3, 0), near(3, 1), hi, grp, sub),
            y_down(near(4, 0), near(4, -1), lo, grp, sub),
            z_up(near(5, 0), hz, kz),
            z_down(near(6, 0), hz, kz),
        ]
        here = pl.ds(8 * x, 8)
        ar, b = co[0, here, :], co[1, here, :]
        s = weighted(q, [co[n, here, :] for n in (2, 3, 4)])
        ars = ar * s
        for n in range(7):
            mid[n, 8 * x + 8 : 8 * x + 16, :] = ars + b * q[n]

        def moved(n, rows):
            return po[n, pl.ds(8 * x + 8 + rows, 8), :]

        hi, lo = row(1, x)
        hz = both_z(1, p, i)
        g = [
            moved(0, 0),
            moved(1, -8),
            moved(2, 8),
            y_down(moved(3, 0), moved(3, -1), lo, grp, sub),
            y_up(moved(4, 0), moved(4, 1), hi, grp, sub),
            z_down(moved(5, 0), hz, kz),
            z_up(moved(6, 0), hz, kz),
        ]
        t = [(s - q[n]) * g[n] for n in range(7)]
        term[here, :] = ((t[0] + t[1]) + (t[2] + t[3])) + ((t[4] + t[5]) + t[6])

    def first(x):
        p, i = x // 32, x % 32

        def near(n, rows):
            return mid[n, pl.ds(8 * x + 8 + rows, 8), :]

        hi, lo = row(2, x)
        hz = both_z(2, p, i)
        q = [
            near(0, 0),
            near(1, 8),
            near(2, -8),
            y_up(near(3, 0), near(3, 1), hi, grp, sub),
            y_down(near(4, 0), near(4, -1), lo, grp, sub),
            z_up(near(5, 0), hz, kz),
            z_down(near(6, 0), hz, kz),
        ]
        here = pl.ds(8 * x, 8)
        ar, b = co[0, here, :], co[1, here, :]
        s = weighted(q, [co[n, here, :] for n in (2, 3, 4)])
        ars = ar * s
        at = pl.ds(8 * i, 8)
        for n in range(7):
            out[n, p, at, :] = ars + b * q[n]
        t = [(s - q[n]) * tg[n, pl.ds(16 * i + p, 8, stride=2), :] for n in range(7)]
        t = ((t[0] + t[1]) + (t[2] + t[3])) + ((t[4] + t[5]) + t[6])
        grad[p, at, :] = co[5, here, :] * (term[here, :] + t)

    middle(0)
    copies = []
    for c in range(CHUNKS):
        for x in range(BLOCK * c, BLOCK * (c + 1)):
            if x + 1 < LAYERS:
                middle(x + 1)
        for x in range(BLOCK * c, BLOCK * (c + 1)):
            first(x)
        p, i = BLOCK * c // 32, BLOCK * c % 32
        rows = pl.ds(8 * i, 8 * BLOCK)
        copies.append(pltpu.make_async_copy(out.at[:, p, rows, :], out_h.at[:, p, rows, :], out_sem.at[c]))
        copies.append(pltpu.make_async_copy(grad.at[p, rows, :], grad_h.at[p, rows, :], grad_sem.at[c]))
        copies[-2].start()
        copies[-1].start()
    for copy in copies:
        copy.wait()


def on_device(nz, populations, adjoint_final, velocity, particle_kappa, solid_label, tile_active):
    def paired(block):
        n = block.shape[0]
        return block.reshape(n, 2, 256, 128).transpose(0, 2, 1, 3).reshape(n, ROWS, 128)

    args = [
        paired(populations), paired(adjoint_final), paired(velocity),
        particle_kappa.reshape(ROWS, 128), solid_label.reshape(ROWS, 128), tile_active.reshape(1, 2),
    ]
    args = [pltpu.with_memory_space_constraint(a, pltpu.HBM) for a in args]
    hbm, vmem = pl.BlockSpec(memory_space=pltpu.HBM), pl.BlockSpec(memory_space=pltpu.VMEM)
    kept = [
        pltpu.VMEM(shape, F32)
        for shape in (
            (7, ROWS + 32, 128), (7, ROWS, 128), (7, ROWS + 16, 128), (6, ROWS, 128),
            (3, LAYERS, 128), (12, 8, 128), (2, 8, 128),
        )
    ]
    messages = [pltpu.VMEM((n, 128), F32) for n in PARTS]
    held = pl.pallas_call(
        functools.partial(exchange, nz),
        out_shape=kept,
        in_specs=[hbm] * 6,
        out_specs=[vmem] * 7,
        scratch_shapes=[
            pltpu.VMEM((7, ROWS, 128), jnp.bfloat16),
            pltpu.VMEM((7, ROWS, 128), jnp.bfloat16),
            pltpu.VMEM((3, ROWS, 128), jnp.bfloat16),
            pltpu.VMEM((ROWS, 128), F32),
            pltpu.VMEM((ROWS, 128), jnp.int32),
            pltpu.SMEM((1, 2), jnp.int32),
            pltpu.VMEM((3, ROWS, 128), F32),
            pltpu.VMEM((5, ROWS, 128), F32),
            pltpu.VMEM((2, ROWS, 128), F32),
            pltpu.VMEM((7, 8, 128), F32),
            *messages,
            *messages,
            pltpu.SemaphoreType.DMA((6,)),
            pltpu.SemaphoreType.DMA((9,)),
            pltpu.SemaphoreType.DMA((9,)),
            pltpu.SemaphoreType.REGULAR,
        ],
        compiler_params=pltpu.CompilerParams(
            collective_id=0, has_side_effects=True, vmem_limit_bytes=24 * 2**20
        ),
        name="exchange",
    )(*args)
    first, gradient = pl.pallas_call(
        finish,
        out_shape=[
            jax.ShapeDtypeStruct((7, 2, 256, 128), F32),
            jax.ShapeDtypeStruct((2, 256, 128), F32),
        ],
        in_specs=[vmem] * 7,
        out_specs=[hbm] * 2,
        scratch_shapes=[
            pltpu.VMEM((7, ROWS + 16, 128), F32),
            pltpu.VMEM((ROWS, 128), F32),
            pltpu.VMEM((7, 2, 256, 128), F32),
            pltpu.VMEM((2, 256, 128), F32),
            pltpu.SemaphoreType.DMA((CHUNKS,)),
            pltpu.SemaphoreType.DMA((CHUNKS,)),
        ],
        compiler_params=pltpu.CompilerParams(vmem_limit_bytes=24 * 2**20),
        name="finish",
    )(*held)
    voxels = EDGE * EDGE * EDGE
    return first.reshape(7, 2, 1, 1, voxels), gradient.reshape(2, 1, 1, voxels)


def solution(mesh):
    spec, one = P(None, "gx", "gy", "gz", None), P("gx", "gy", "gz", None)
    return jax.shard_map(
        functools.partial(on_device, mesh.shape["gz"]),
        mesh=mesh,
        in_specs=(spec, spec, spec, one, one, P("gx", "gy", "gz")),
        out_specs=(spec, one),
        check_vma=False,
    )
```

```python
import functools

import jax
import jax.numpy as jnp
from jax import lax
from jax.experimental import pallas as pl
from jax.experimental.pallas import tpu as pltpu
from jax.sharding import PartitionSpec as P

EDGE = 32
FLUID_KAPPA = 1.0 / 6.0
MESH = pl.DeviceIdType.MESH
F32 = jnp.float32
LAYERS = 2 * EDGE
ROWS = 8 * LAYERS
PARTS = (48, 73, 74, 74, 2, 8, 8, 10, 10)


def masks():
    lane = lax.broadcasted_iota(jnp.int32, (8, 128), 1)
    sub = lax.broadcasted_iota(jnp.int32, (8, 128), 0)
    return lane & 31, lane >> 5, sub


def pick(flag, yes, no):
    return jnp.where(jnp.broadcast_to(flag, (8, 128)), yes, no)


def z_up(v, halo, kz):
    return jnp.where(kz == 31, halo, pltpu.roll(v, 127, 1))


def z_down(v, halo, kz):
    return jnp.where(kz == 0, halo, pltpu.roll(v, 1, 1))


def y_up(v, after, halo, grp, sub):
    return pltpu.roll(jnp.where(grp == 0, jnp.where(sub == 7, halo, after), v), 96, 1)


def y_down(v, before, halo, grp, sub):
    return pltpu.roll(jnp.where(grp == 3, jnp.where(sub == 0, halo, before), v), 32, 1)


def weighted(q, d):
    even = (q[1] + q[2]) + (q[3] + q[4]) + (q[5] + q[6])
    odd = d[0] * (q[1] - q[2]) + d[1] * (q[3] - q[4]) + d[2] * (q[5] - q[6])
    return 0.25 * q[0] + 0.125 * even + 0.5 * odd


def part(n):
    return slice(8 * n, 8 * n + 8)


def tile8(row):
    return pl.ds(pl.multiple_of(row, 8), 8)


def exchange(
    nz, pop_h, fin_h, vel_h, kap_h, sol_h, act_h,
    tf, tg, po, co, yh, zh, xh,
    popb, finb, velb, kapb, solb, actb, tv, zm, ym, zp,
    s0, s1, s2, s3, s4, s5, s6, s7, s8, r0, r1, r2, r3, r4, r5, r6, r7, r8,
    load_sem, send_sem, recv_sem, ready,
):
    sends = (s0, s1, s2, s3, s4, s5, s6, s7, s8)
    gets = (r0, r1, r2, r3, r4, r5, r6, r7, r8)
    gx, gy, gz = lax.axis_index("gx"), lax.axis_index("gy"), lax.axis_index("gz")
    ox, oy, up, down = 1 - gx, 1 - gy, gz + 1, gz - 1
    peers = (
        (ox, gy, gz), (gx, oy, gz), (gx, gy, up), (gx, gy, down), (ox, oy, gz),
        (ox, gy, up), (ox, gy, down), (gx, oy, up), (gx, oy, down),
    )
    has_up, has_down = gz < nz - 1, gz > 0
    exists = (None, None, has_up, has_down, None, has_up, has_down, has_up, has_down)
    root = (gx == 0) & (gy == 0) & (gz == 0)
    other = jnp.logical_not(root)
    to_root = [(x == 0) & (y == 0) & (z == 0) for x, y, z in peers]

    def guarded(k, act, also=None):
        flag = exists[k]
        if also is not None:
            flag = also if flag is None else flag & also
        if flag is None:
            act()
        else:
            pl.when(flag)(act)

    barrier = pltpu.get_barrier_semaphore()

    def signal(k, semaphore):
        return lambda: pl.semaphore_signal(semaphore, inc=1, device_id=peers[k], device_id_type=MESH)

    for k in range(9):
        guarded(k, signal(k, barrier), other)
    count = 3 + 3 * has_up.astype(jnp.int32) + 3 * has_down.astype(jnp.int32)
    near_root = functools.reduce(jnp.logical_or, to_root)
    loads = [
        pltpu.make_async_copy(src, dst, load_sem.at[n])
        for n, (src, dst) in enumerate(
            ((act_h, actb), (fin_h, finb), (vel_h, velb), (kap_h, kapb), (sol_h, solb), (pop_h, popb))
        )
    ]
    for copy in loads:
        copy.start()

    @pl.when(root)
    def _():
        pl.semaphore_wait(barrier, count)
        for k in range(9):
            guarded(k, signal(k, ready))

    lands = (0, 1, 3, 2, 4, 6, 5, 8, 7)
    copies = [
        pltpu.make_async_remote_copy(
            src_ref=sends[k], dst_ref=gets[lands[k]], send_sem=send_sem.at[k], recv_sem=recv_sem.at[lands[k]],
            device_id=peers[k], device_id_type=MESH,
        )
        for k in range(9)
    ]

    kz, grp, sub = masks()
    zero = jnp.zeros((8, 128), F32)
    s_e, g_e = 7 * oy, 3 * oy
    s_c = lax.rem(s_e + 4, 8)
    i_e, p_e = 31 * ox, ox
    sgx, sgy = (1 - 2 * gx).astype(F32), (1 - 2 * gy).astype(F32)
    first_x, first_y = gx == 0, gy == 0
    fx, fy = 1 + ox, 3 + oy
    zsign = jnp.where(kz == 0, -0.5, 0.5)

    @pl.when(gz == nz - 1)
    def _():
        for k in (2, 5, 7):
            gets[k][...] = jnp.zeros_like(gets[k])

    @pl.when(gz == 0)
    def _():
        for k in (3, 6, 8):
            gets[k][...] = jnp.zeros_like(gets[k])

    loads[1].wait()
    for n in range(7):
        tf[n, 16 : 16 + ROWS, :] = finb[n].astype(F32)
    for n in (1, 2):
        tf[n, pl.ds(0, 8, stride=2), :] = zero
        tf[n, pl.ds(1, 8, stride=2), :] = tf[n, pl.ds(16 * 32, 8, stride=2), :]
        tf[n, pl.ds(16 * 33, 8, stride=2), :] = tf[n, pl.ds(16 + 1, 8, stride=2), :]
        tf[n, pl.ds(16 * 33 + 1, 8, stride=2), :] = zero
        po[n, 0:8, :] = zero
        po[n, ROWS + 8 : ROWS + 16, :] = zero
    def pack_y(read):
        out = []
        for h in range(2):
            v = zero
            for g in range(4):
                rows = read(32 * h + 8 * g, h, 8 * g)
                v = jnp.where(grp == g, pltpu.roll(rows, lax.rem(32 * (g - g_e) + 128, 128), 1), v)
            out.append(v)
        return out

    def every8(ref, n):
        return lambda x, h, i: ref[n, pl.ds(8 * x + s_e, 8, stride=8), :]


    own_face_y = pack_y(lambda x, h, i: tf[fy, pl.ds(16 * (i + 1) + h + 2 * s_e, 8, stride=16), :])

    def gather(n, first, count):
        for p in range(2):
            low, high = zp[4 * n + 2 * p], zp[4 * n + 2 * p + 1]
            for k in range(count):
                i = first + k
                v = pltpu.roll(zm[n, tile8(256 * p + 8 * i), :], i, 1)
                low = jnp.where(kz == i, v, low)
                high = jnp.where(kz == ((i + 31) & 31), v, high)
            zp[4 * n + 2 * p], zp[4 * n + 2 * p + 1] = low, high

    zp[4:20] = jnp.zeros((16, 8, 128), F32)
    faces = [zero] * 4
    for i in range(32):
        for p in range(2):
            at = pl.ds(16 * (i + 1) + p, 8, stride=2)
            v = jnp.where(kz == 0, tf[5, at, :], tf[6, at, :])
            zm[0, 256 * p + 8 * i : 256 * p + 8 * i + 8, :] = v
            v = pltpu.roll(v, i, 1)
            faces[2 * p] = jnp.where(kz == i, v, faces[2 * p])
            faces[2 * p + 1] = jnp.where(kz == (i + 31) % 32, v, faces[2 * p + 1])
    for v in range(2):
        s3[part(v)] = faces[2 * v]
        s2[part(v)] = pltpu.roll(faces[2 * v + 1], 97, 1)
    zy = pack_y(every8(zm, 0))
    loads[2].wait()
    for n in range(3):
        tv[n] = velb[n].astype(F32)
    loads[5].wait()
    for n in range(7):
        tg[n] = popb[n].astype(F32)
    loads[0].wait()
    loads[3].wait()
    loads[4].wait()
    active = (actb[0, 0].astype(F32), actb[0, 1].astype(F32))

    def cell(i, p, a):
        near = [tf[n, pl.ds(16 * (i + 1) + p, 8, stride=2), :] for n in (0, 3, 4, 5, 6)]
        q = [
            near[0],
            tf[1, pl.ds(16 * (i + 2) + p, 8, stride=2), :],
            tf[2, pl.ds(16 * i + p, 8, stride=2), :],
            y_up(near[1], tf[3, pl.ds(16 * (i + 1) + p + 2, 8, stride=2), :], zero, grp, sub),
            y_down(near[2], tf[4, pl.ds(16 * (i + 1) + p - 2, 8, stride=2), :], zero, grp, sub),
            z_up(near[3], zero, kz),
            z_down(near[4], zero, kz),
        ]
        here = tile8(256 * p + 8 * i)
        solid = solb[here, :] > 0
        kappa = jnp.where(solid, kapb[here, :], FLUID_KAPPA)
        rate = 1.0 / (4.0 * kappa + 0.5)
        ar = a * rate
        b = a - ar
        d = [jnp.where(solid, 0.0, tv[n, pl.ds(16 * i + p, 8, stride=2), :]) for n in range(3)]
        return near, q, solid, rate, ar, b, d, ar * weighted(q, d)

    def weights(i, p, ar):
        g = [tg[n, pl.ds(16 * i + p, 8, stride=2), :] for n in range(7)]
        return g, ar * (((g[0] + g[1]) + (g[2] + g[3])) + ((g[4] + g[5]) + g[6]))

    def layer(i, p, a):
        x = 32 * p + i
        near, q, solid, rate, ar, b, d, ars = cell(i, p, a)
        here = tile8(8 * x)
        for n, c in enumerate((ar, b, d[0], d[1], d[2])):
            co[n, here, :] = c
        g, w = weights(i, p, ar)
        even = 0.125 * w
        odd = 0.5 * (w * d[2])
        post_5, post_6 = b * g[5] + (even + odd), b * g[6] + (even - odd)
        to_y = ar * (0.125 + 0.5 * sgy * d[1])
        bottom = kz == 0
        zm[1, here, :] = jnp.where(bottom, post_6, post_5)
        zm[2, here, :] = ars + b * jnp.where(bottom, q[5], q[6])
        zm[3, here, :] = ar * (0.125 + zsign * d[2])
        zm[4, here, :] = jnp.where(sub == s_e, pick(first_y, near[2], near[1]), pltpu.roll(to_y, 4, 0))
        ym[0, here, :] = ars + b * pick(first_y, q[4], q[3])
        ym[1, here, :] = to_y
        ym[2, here, :] = b * pick(first_y, g[3], g[4]) + (even + 0.5 * (w * (sgy * d[1])))
        return near, q, ar, b, d, ars, g, w

    a_e = jnp.where(first_x, active[1], active[0])
    near, q, ar, b, d, ars, g, w = layer(i_e, p_e, a_e)
    x_e = 63 * ox
    here_e = tile8(8 * x_e)
    to_x = ar * (0.125 + 0.5 * sgx * d[0])
    own_x = tf[fx, pl.ds(16 * (i_e + 1) + p_e, 8, stride=2), :]
    own_y = pick(first_y, near[2], near[1])
    s0[part(0)] = own_x
    s0[part(1)] = b * pick(first_x, g[1], g[2]) + (0.125 * w + 0.5 * (w * (sgx * d[0])))
    s0[part(2)] = ars + b * pick(first_x, q[2], q[1])
    s0[part(3)] = to_x
    s0[part(4)] = ym[1, here_e, :]
    s0[part(5)] = zm[3, here_e, :]
    pl.when(root)(copies[0].start)

    def block(first):
        for k in range(8):
            layer(first + k, 0, active[0])
            layer(first + k, 1, active[1])

    def sweep(c, carry):
        for n in range(1, 5):
            gather(n, 8 * c - 8, 8)
        block(8 * c)
        return carry

    block(0)
    lax.fori_loop(1, 4, sweep, 0)
    for n in range(1, 5):
        gather(n, 24, 8)

    packs = (
        own_face_y,
        pack_y(every8(ym, 2)),
        pack_y(every8(ym, 0)),
        pack_y(every8(ym, 1)),
        pack_y(every8(zm, 3)),
    )
    for n, pair in enumerate(packs[:4]):
        s1[part(2 * n)] = pair[0]
        s1[part(2 * n + 1)] = pair[1]
    s1[part(8)] = jnp.where((kz == 7) | (kz == 8), pltpu.roll(packs[4][1], 8, 1), packs[4][0])

    def shifted(v, lanes):
        return pltpu.roll(v, lax.rem(lanes + 256, 128), 1)

    zp[0] = shifted(to_x, 32 * (3 * ox - g_e))
    s1[72:73, :] = zp[0, pl.ds(s_e, 1), :]

    for n in range(1, 4):
        for k, (msg, v) in enumerate(((s3, 0), (s2, 0), (s3, 1), (s2, 1))):
            packed = zp[4 * n + k]
            msg[part(2 * n + v)] = packed if k % 2 == 0 else pltpu.roll(packed, 97, 1)
    for v in range(2):
        zp[21 + v] = pltpu.roll(zp[17 + 2 * v], 97, 1)
    for msg, other_msg, base, step in ((s3, s8, 16, 2), (s2, s7, 21, 1)):
        for h in range(2):
            msg[72 + h : 73 + h, :] = zp[base + step * h, pl.ds(s_c, 1), :]
            other_msg[8 + h : 9 + h, :] = zp[base + step * h, pl.ds(s_e, 1), :]
    s3[part(8)] = shifted(to_x, i_e)
    s2[part(8)] = shifted(to_x, i_e - 31)

    s_o, g_o = 7 * gy, 3 * gy
    zp[1] = jnp.where(grp == g_o, shifted(own_y, 32 * (g_o - g_e)), 0.0)
    zp[2] = jnp.where(grp == 3 * gx, shifted(own_x, 32 * (3 * gx - g_e)), 0.0)
    s4[0:1, :] = zp[1, pl.ds(s_e, 1), :]
    s4[1:2, :] = zp[2, pl.ds(s_e, 1), :]
    z_e = zm[0, here_e, :]
    s6[...] = jnp.where(kz == 16, pltpu.roll(own_x, 16, 1), pltpu.roll(z_e, 31, 1))
    s5[...] = jnp.where(kz == 16, pltpu.roll(own_x, 113, 1), pltpu.roll(z_e, 97, 1))
    s8[0:8, :] = jnp.where(kz == 7, pltpu.roll(zy[1], 39, 1), pltpu.roll(zy[0], 31, 1))
    s7[0:8, :] = jnp.where(kz == 8, pltpu.roll(zy[1], 105, 1), pltpu.roll(zy[0], 97, 1))

    order = (4, 5, 6, 7, 8, 1, 2, 3, 0)

    @pl.when(root)
    def _():
        for k in order[:-1]:
            guarded(k, copies[k].start)

    @pl.when(other)
    def _():
        pl.semaphore_wait(barrier, count - near_root.astype(jnp.int32))
        for k in order:
            guarded(k, copies[k].start, jnp.logical_not(to_root[k]))

    @pl.when(near_root)
    def _():
        pl.semaphore_wait(ready, 1)
        for k in order:
            pl.when(to_root[k])(copies[k].start)

    def rest(i, p):
        x = 32 * p + i
        here = tile8(8 * x)
        padded = tile8(8 * x + 8)
        ar, b = co[0, here, :], co[1, here, :]
        solid = solb[here, :] > 0
        co[5, here, :] = jnp.where(solid, -4.0 * ar * ar, 0.0)
        g, w = weights(i, p, ar)
        po[0, padded, :] = b * g[0] + 0.25 * w
        even = 0.125 * w
        for n in range(3):
            odd = 0.5 * (w * co[2 + n, here, :])
            po[2 * n + 1, padded, :] = b * g[2 * n + 1] + (even + odd)
            po[2 * n + 2, padded, :] = b * g[2 * n + 2] + (even - odd)

    def finish_rest(c, carry):
        for k in range(8):
            rest(8 * c + k, 0)
            rest(8 * c + k, 1)
        return carry

    lax.fori_loop(0, 4, finish_rest, 0)

    def arrival(k):
        return pltpu.make_async_remote_copy(
            src_ref=sends[lands[k]], dst_ref=gets[k], send_sem=send_sem.at[k], recv_sem=recv_sem.at[k],
            device_id=peers[k], device_id_type=MESH,
        )

    for k in range(9):
        guarded(k, lambda k=k: arrival(k).wait_recv())

    hi_x, lo_x = ox.astype(F32), gx.astype(F32)

    def spread(row):
        return jnp.broadcast_to(row, (8, 128))

    top, bottom = kz == 31, kz == 0
    line_y = jnp.where(sub == 7 * ox, spread(r4[1:2, :]), 0.0)
    mid_y = []
    for h in range(2):
        edge = [r1[part(8)], r7[0:8, :], r8[0:8, :]]
        if h == 1:
            edge = [pltpu.roll(v, 120, 1) for v in edge]
        m = r1[part(4 + h)] + r1[part(6 + h)] * s1[part(h)]
        m = m + edge[0] * (jnp.where(top, edge[1], 0.0) + jnp.where(bottom, edge[2], 0.0))
        mid_y.append(m + (hi_x if h == 1 else lo_x) * (spread(r1[72:73, :]) * line_y))
    for n, pair in enumerate(((r1[part(0)], r1[part(1)]), (r1[part(2)], r1[part(3)]), mid_y)):
        for h in range(2):
            for g in range(4):
                yh[n, pl.ds(32 * h + 8 * g, 8), :] = pltpu.roll(pair[h], lax.rem(32 * (g_o - g) + 128, 128), 1)
    corner = (sub == s_e) & (grp == g_e)
    for base, msg, line, cross, own in ((0, r2, r7, r5, s2), (6, r3, r8, r6, s3)):
        line_z = jnp.where(kz == i_e, shifted(cross[...], i_e - 16), 0.0)
        for v in range(2):
            side = hi_x if v == 1 else lo_x
            m = msg[part(4 + v)] + msg[part(6 + v)] * own[part(v)] + side * (msg[part(8)] * line_z)
            f = shifted(spread(line[8 + v : 9 + v, :]), 32 * (g_e - g_o))
            m = m + jnp.where(corner, spread(msg[72 + v : 73 + v, :]) * f, 0.0)
            for n, halo in enumerate((msg[part(v)], msg[part(2 + v)], m)):
                zh[base + 2 * n + v] = halo if base == 0 else pltpu.roll(halo, 97, 1)
    mid_x = r0[part(2)] + r0[part(3)] * s0[part(0)]
    mid_x = mid_x + r0[part(4)] * jnp.where(sub == s_e, spread(r4[0:1, :]), 0.0)
    mid_x = mid_x + r0[part(5)] * (jnp.where(top, r5[...], 0.0) + jnp.where(bottom, r6[...], 0.0))
    xh[0] = hi_x * mid_x
    xh[1] = lo_x * mid_x
    tf[1, pl.ds(16 * 33 + 1, 8, stride=2), :] = hi_x * r0[part(0)]
    tf[2, pl.ds(0, 8, stride=2), :] = lo_x * r0[part(0)]
    po[2, ROWS + 8 : ROWS + 16, :] = hi_x * r0[part(1)]
    po[1, 0:8, :] = lo_x * r0[part(1)]
    for k in range(9):
        guarded(k, copies[k].wait_send)


BLOCK = 16
CHUNKS = LAYERS // BLOCK


def finish(tf, tg, po, co, yh, zh, xh, out_h, grad_h, mid, term, out, grad, out_sem, grad_sem):
    kz, grp, sub = masks()
    gy = lax.axis_index("gy")
    hi_y, lo_y = (1 - gy).astype(F32), gy.astype(F32)

    def row(n, x):
        r = jnp.broadcast_to(yh[n, x : x + 1, :], (8, 128))
        return hi_y * r, lo_y * r

    def both_z(n, p, i):
        return pltpu.roll(jnp.where(kz == i, zh[2 * n + p], zh[6 + 2 * n + p]), 31 - i, 1)

    mid[1, ROWS + 8 : ROWS + 16, :] = xh[0]
    mid[2, 0:8, :] = xh[1]

    def middle(x):
        p, i = x // 32, x % 32

        def near(n, rows):
            return tf[n, pl.ds(16 * (i + 1) + p + 2 * rows, 8, stride=2), :]

        hi, lo = row(0, x)
        hz = both_z(0, p, i)
        q = [
            near(0, 0),
            near(1, 8),
            near(2, -8),
            y_up(near(3, 0), near(3, 1), hi, grp, sub),
            y_down(near(4, 0), near(4, -1), lo, grp, sub),
            z_up(near(5, 0), hz, kz),
            z_down(near(6, 0), hz, kz),
        ]
        here = pl.ds(8 * x, 8)
        ar, b = co[0, here, :], co[1, here, :]
        s = weighted(q, [co[n, here, :] for n in (2, 3, 4)])
        ars = ar * s
        for n in range(7):
            mid[n, 8 * x + 8 : 8 * x + 16, :] = ars + b * q[n]

        def moved(n, rows):
            return po[n, pl.ds(8 * x + 8 + rows, 8), :]

        hi, lo = row(1, x)
        hz = both_z(1, p, i)
        g = [
            moved(0, 0),
            moved(1, -8),
            moved(2, 8),
            y_down(moved(3, 0), moved(3, -1), lo, grp, sub),
            y_up(moved(4, 0), moved(4, 1), hi, grp, sub),
            z_down(moved(5, 0), hz, kz),
            z_up(moved(6, 0), hz, kz),
        ]
        t = [(s - q[n]) * g[n] for n in range(7)]
        term[here, :] = ((t[0] + t[1]) + (t[2] + t[3])) + ((t[4] + t[5]) + t[6])

    def first(x):
        p, i = x // 32, x % 32

        def near(n, rows):
            return mid[n, pl.ds(8 * x + 8 + rows, 8), :]

        hi, lo = row(2, x)
        hz = both_z(2, p, i)
        q = [
            near(0, 0),
            near(1, 8),
            near(2, -8),
            y_up(near(3, 0), near(3, 1), hi, grp, sub),
            y_down(near(4, 0), near(4, -1), lo, grp, sub),
            z_up(near(5, 0), hz, kz),
            z_down(near(6, 0), hz, kz),
        ]
        here = pl.ds(8 * x, 8)
        ar, b = co[0, here, :], co[1, here, :]
        s = weighted(q, [co[n, here, :] for n in (2, 3, 4)])
        ars = ar * s
        at = pl.ds(8 * i, 8)
        for n in range(7):
            out[n, p, at, :] = ars + b * q[n]
        t = [(s - q[n]) * tg[n, pl.ds(16 * i + p, 8, stride=2), :] for n in range(7)]
        t = ((t[0] + t[1]) + (t[2] + t[3])) + ((t[4] + t[5]) + t[6])
        grad[p, at, :] = co[5, here, :] * (term[here, :] + t)

    middle(0)
    copies = []
    for c in range(CHUNKS):
        for x in range(BLOCK * c, BLOCK * (c + 1)):
            if x + 1 < LAYERS:
                middle(x + 1)
        for x in range(BLOCK * c, BLOCK * (c + 1)):
            first(x)
        p, i = BLOCK * c // 32, BLOCK * c % 32
        rows = pl.ds(8 * i, 8 * BLOCK)
        copies.append(pltpu.make_async_copy(out.at[:, p, rows, :], out_h.at[:, p, rows, :], out_sem.at[c]))
        copies.append(pltpu.make_async_copy(grad.at[p, rows, :], grad_h.at[p, rows, :], grad_sem.at[c]))
        copies[-2].start()
        copies[-1].start()
    for copy in copies:
        copy.wait()


def on_device(nz, populations, adjoint_final, velocity, particle_kappa, solid_label, tile_active):
    def paired(block):
        n = block.shape[0]
        return block.reshape(n, 2, 256, 128).transpose(0, 2, 1, 3).reshape(n, ROWS, 128)

    args = [
        paired(populations), paired(adjoint_final), paired(velocity),
        particle_kappa.reshape(ROWS, 128), solid_label.reshape(ROWS, 128), tile_active.reshape(1, 2),
    ]
    args = [pltpu.with_memory_space_constraint(a, pltpu.HBM) for a in args]
    hbm, vmem = pl.BlockSpec(memory_space=pltpu.HBM), pl.BlockSpec(memory_space=pltpu.VMEM)
    kept = [
        pltpu.VMEM(shape, F32)
        for shape in (
            (7, ROWS + 32, 128), (7, ROWS, 128), (7, ROWS + 16, 128), (6, ROWS, 128),
            (3, LAYERS, 128), (12, 8, 128), (2, 8, 128),
        )
    ]
    messages = [pltpu.VMEM((n, 128), F32) for n in PARTS]
    held = pl.pallas_call(
        functools.partial(exchange, nz),
        out_shape=kept,
        in_specs=[hbm] * 6,
        out_specs=[vmem] * 7,
        scratch_shapes=[
            pltpu.VMEM((7, ROWS, 128), jnp.bfloat16),
            pltpu.VMEM((7, ROWS, 128), jnp.bfloat16),
            pltpu.VMEM((3, ROWS, 128), jnp.bfloat16),
            pltpu.VMEM((ROWS, 128), F32),
            pltpu.VMEM((ROWS, 128), jnp.int32),
            pltpu.SMEM((1, 2), jnp.int32),
            pltpu.VMEM((3, ROWS, 128), F32),
            pltpu.VMEM((5, ROWS, 128), F32),
            pltpu.VMEM((3, ROWS, 128), F32),
            pltpu.VMEM((23, 8, 128), F32),
            *messages,
            *messages,
            pltpu.SemaphoreType.DMA((6,)),
            pltpu.SemaphoreType.DMA((9,)),
            pltpu.SemaphoreType.DMA((9,)),
            pltpu.SemaphoreType.REGULAR,
        ],
        compiler_params=pltpu.CompilerParams(
            collective_id=0, has_side_effects=True, vmem_limit_bytes=24 * 2**20
        ),
        name="exchange",
    )(*args)
    first, gradient = pl.pallas_call(
        finish,
        out_shape=[
            jax.ShapeDtypeStruct((7, 2, 256, 128), F32),
            jax.ShapeDtypeStruct((2, 256, 128), F32),
        ],
        in_specs=[vmem] * 7,
        out_specs=[hbm] * 2,
        scratch_shapes=[
            pltpu.VMEM((7, ROWS + 16, 128), F32),
            pltpu.VMEM((ROWS, 128), F32),
            pltpu.VMEM((7, 2, 256, 128), F32),
            pltpu.VMEM((2, 256, 128), F32),
            pltpu.SemaphoreType.DMA((CHUNKS,)),
            pltpu.SemaphoreType.DMA((CHUNKS,)),
        ],
        compiler_params=pltpu.CompilerParams(vmem_limit_bytes=24 * 2**20),
        name="finish",
    )(*held)
    voxels = EDGE * EDGE * EDGE
    return first.reshape(7, 2, 1, 1, voxels), gradient.reshape(2, 1, 1, voxels)


def solution(mesh):
    spec, one = P(None, "gx", "gy", "gz", None), P("gx", "gy", "gz", None)
    return jax.shard_map(
        functools.partial(on_device, mesh.shape["gz"]),
        mesh=mesh,
        in_specs=(spec, spec, spec, one, one, P("gx", "gy", "gz")),
        out_specs=(spec, one),
        check_vma=False,
    )
```
